32 devices in a mesh: tm: 4 (over y, x), space: 8 (over z, core).
Axes of the slice: x: 2, y: 2, z: 4, core: 2. Of those that a mesh axis runs over, the one named last changes fastest.
Arguments:
- state: float32 [4, 64, 32, 256], P('tm', 'space'), may hold values from -2 to 2
- initial: float32 [64, 32, 256], P('space'), may hold values from -2.5 to 2.5
- labels: int32 [64, 32, 256], P('space'), may hold values from 0 to 15
- mobility_table: float32 [16], replicated, may hold values from 0.5 to 2
Outputs:
- new_state: float32 [4, 64, 32, 256], P('tm', 'space')
The draws below stay inside these ranges and needn't reach their ends.
All inputs are finite; a program needn't handle non-finite values.
Results may differ from the reference program's by a relative error of at most 0.0003.
Values sent between devices are 32-bit elements; how exact they have to be, the bound alone decides.
A program may use at most 64 MiB of HBM per device.

```python
import math
import jax
import jax.numpy as jnp
from jax import lax

NX = 32
NY = 256
SWEEPS = 8
GRAINS = 16
STEPS = 4
NZ = 64


def draw_state(key, part):
    full_shape = (STEPS, NZ, NX, NY)
    values = jnp.clip(0.7 * jax.random.normal(key, full_shape, jnp.float32), -2.0, 2.0)
    return values


def touch_ends(values, key, smallest, high):
    shape = values.shape
    spot = [jax.random.randint(jax.random.fold_in(key, axis), (), 0, shape[axis]) for axis in range(len(shape))]
    values = values.at[tuple(spot)].set(smallest)
    longest = shape.index(max(shape))
    spot[longest] = (spot[longest] + 1) % shape[longest]
    return values.at[tuple(spot)].set(high)


def block_levels(stream_key, extent, cuts, least, largest):
    gain, own = 1.0, jax.random.fold_in(stream_key, 6)
    for dim, shards_of in cuts:
        draws = jnp.exp(jax.random.uniform(jax.random.fold_in(own, dim), (shards_of,), jnp.float32, least / len(cuts), largest / len(cuts)))
        gain = gain * jnp.repeat(draws, extent[dim] // shards_of).reshape([-1 if axis == dim else 1 for axis in range(len(extent))])
    return gain


def bell_draw(own_key, dims, width, most, pieces=(), kind=jnp.bfloat16):
    array = jax.random.normal(own_key, dims, jnp.float32) * width
    if len(pieces) > 0:
        array = block_levels(own_key, dims, pieces, -0.22, 0.18) * array
    return jnp.clip(array, min=-most, max=most).astype(kind)


def setup_inputs(seed: int = 0) -> dict:
    arg_keys = jax.random.split(jax.random.key(seed), 5)
    state = draw_state(jax.random.fold_in(arg_keys[4], 71), 0)
    initial = bell_draw(arg_keys[1], (NZ, NX, NY), 0.7, 2.5, ((0, 8),), jnp.float32)
    labels = touch_ends(jax.random.randint(arg_keys[2], (NZ, NX, NY), 0, GRAINS), jax.random.fold_in(arg_keys[2], 1), 0, GRAINS - 1).astype(jnp.int32)
    mobility_table = jnp.clip(jnp.exp(jax.random.uniform(arg_keys[3], (GRAINS,), jnp.float32, math.log(0.5), math.log(2.0))), 0.5, 2.0)
    return {"state": state, "initial": initial, "labels": labels, "mobility_table": mobility_table}


alpha_wrap = 0.1
tau_step = 0.25
kappa_grad = 4.0
diag_extra = 6.5


def neighbours(grid_field):
    summed = jnp.roll(grid_field, 1, 0) + jnp.roll(grid_field, -1, 0)
    summed = summed + jnp.roll(grid_field, 1, 1) + jnp.roll(grid_field, -1, 1)
    return summed + jnp.roll(grid_field, 1, 2) + jnp.roll(grid_field, -1, 2)


def mobility_of(labels, rate_table):
    def add_grain(grain_id, summed):
        return summed + jnp.where(labels == grain_id, rate_table[grain_id], jnp.zeros((), rate_table.dtype))
    return lax.fori_loop(0, GRAINS, add_grain, jnp.zeros(labels.shape, rate_table.dtype))


def reference(state, initial, labels, mobility_table):
    highest = lax.Precision.HIGHEST
    mobility = mobility_of(labels, mobility_table)
    previous = jnp.concatenate([initial[None], state[:-1]], axis=0)

    def residual_of(both_steps):
        current, earlier_step = both_steps
        laplacian = neighbours(current) - 6.0 * current
        return current - earlier_step + tau_step * mobility * (current * current * current - current - kappa_grad * laplacian)

    residual = lax.map(residual_of, (state, previous))
    time_axis = jnp.arange(STEPS)
    gamma_scale = alpha_wrap ** (time_axis.astype(state.dtype) / STEPS)
    phase_angle = ((time_axis[:, None] * time_axis[None, :]) % STEPS).astype(state.dtype) * (2.0 * math.pi / STEPS)
    cos_table = jnp.cos(phase_angle)
    sin_table = jnp.sin(phase_angle)
    scaled = residual * gamma_scale[:, None, None, None]
    rhs_real_all = jnp.einsum("kt,tzxy->kzxy", cos_table, scaled, precision=highest)
    rhs_imag_all = -jnp.einsum("kt,tzxy->kzxy", sin_table, scaled, precision=highest)
    beta_root = alpha_wrap ** (1.0 / STEPS)

    def solve_one(per_freq):
        rhs_real, rhs_imag, freq_index = per_freq
        freq_angle = freq_index.astype(state.dtype) * (2.0 * math.pi / STEPS)
        diag_real = 1.0 - beta_root * jnp.cos(freq_angle) + diag_extra * mobility
        diag_imag = beta_root * jnp.sin(freq_angle)
        magnitude = diag_real * diag_real + diag_imag * diag_imag
        inv_real = diag_real / magnitude
        inv_imag = -diag_imag / magnitude
        sol_real = rhs_real * inv_real - rhs_imag * inv_imag
        sol_imag = rhs_real * inv_imag + rhs_imag * inv_real
        for sweep_index in range(SWEEPS):
            sum_real = rhs_real + mobility * neighbours(sol_real)
            sum_imag = rhs_imag + mobility * neighbours(sol_imag)
            sol_real, sol_imag = sum_real * inv_real - sum_imag * inv_imag, sum_real * inv_imag + sum_imag * inv_real
        return sol_real, sol_imag

    sol_real_all, sol_imag_all = lax.map(solve_one, (rhs_real_all, rhs_imag_all, time_axis))
    back_sum = jnp.einsum("nk,kzxy->nzxy", cos_table, sol_real_all, precision=highest) - jnp.einsum("nk,kzxy->nzxy", sin_table, sol_imag_all, precision=highest)
    correction = back_sum / (STEPS * gamma_scale)[:, None, None, None]
    return state - correction
```

```python
import functools
import math

import jax
import jax.numpy as jnp
from jax import lax
from jax.experimental import pallas as pl
from jax.experimental.pallas import tpu as pltpu
from jax.sharding import PartitionSpec as P

MESH = pl.DeviceIdType.MESH
SWEEPS = 8
GRAINS = 16


alpha_wrap = 0.1
tau_step = 0.25
kappa_grad = 4.0
diag_extra = 6.5


def passed_along(array, axis, by):
    devices = lax.axis_size(axis)
    pairs = [(i, i + by) for i in range(devices) if 0 <= i + by < devices]
    return lax.ppermute(array, axis, pairs)


def extended(cells, sides, width):
    for axis, dim in sides:
        count = lax.axis_size(axis)
        head = lax.slice_in_dim(cells, 0, width, axis=dim)
        tail = lax.slice_in_dim(cells, cells.shape[dim] - width, cells.shape[dim], axis=dim)
        cells = jnp.concatenate(
            [
                lax.ppermute(tail, axis, [(i, (i + 1) % count) for i in range(count)]),
                cells,
                lax.ppermute(head, axis, [((i + 1) % count, i) for i in range(count)]),
            ],
            axis=dim,
        )
    return cells


def partner_2(value, axis, apart):
    mask = 2**apart
    pairs = [(source, source ^ mask) for source in range(lax.axis_size(axis))]
    return lax.ppermute(value, axis, pairs)


def plane_sum(grid_field):
    summed = jnp.roll(grid_field, 1, -2) + jnp.roll(grid_field, -1, -2)
    return summed + jnp.roll(grid_field, 1, -1) + jnp.roll(grid_field, -1, -1)


def mobility_of(labels, rate_table):

    def add_grain(grain_id, summed):
        return summed + jnp.where(
            labels == grain_id, rate_table[grain_id], jnp.zeros((), rate_table.dtype)
        )

    return lax.fori_loop(0, GRAINS, add_grain, jnp.zeros(labels.shape, rate_table.dtype))


def complex_times(left_val, right_val):
    return jnp.stack(
        [
            left_val[0] * right_val[0] - left_val[1] * right_val[1],
            left_val[0] * right_val[1] + left_val[1] * right_val[0],
        ]
    )


def sweep_once(padded, spectral_rhs, inverse_diag, mobility):
    middle = padded[:, 1:-1]
    summed = spectral_rhs + mobility * (padded[:, 2:] + padded[:, :-2] + plane_sum(middle))
    return complex_times(summed, inverse_diag)


def inverse_of(mobility, freq_angle, beta_root):
    diag_real = 1.0 - beta_root * jnp.cos(freq_angle) + diag_extra * mobility
    diag_imag = beta_root * jnp.sin(freq_angle)
    magnitude = diag_real * diag_real + diag_imag * diag_imag
    return jnp.stack([diag_real / magnitude, -diag_imag / magnitude])


def shards(state, initial, labels, mobility_table):
    time_count = lax.axis_size("tm")
    section_count = time_count.bit_length() - 1
    time_index = lax.axis_index("tm")
    index_float = time_index.astype(jnp.float32)
    angle_unit = 2.0 * math.pi / time_count
    gamma_here = alpha_wrap ** (index_float / time_count)
    current = state[0]
    mobility = mobility_of(labels, mobility_table)
    earlier = passed_along(state, "tm", 1)
    earlier_step = jnp.where(time_index == 0, initial, earlier[0])
    padded = extended(current, (("space", 0),), 1)
    laplacian = padded[2:] + padded[:-2] + plane_sum(current) - 6.0 * current
    residual = (
        current
        - earlier_step
        + tau_step * mobility * (current * current * current - current - kappa_grad * laplacian)
    )
    top_bit = section_count - 1
    half_span = 2**top_bit
    local_part = residual * gamma_here
    partner = partner_2(local_part, "tm", top_bit)
    upper_half = time_index // half_span % 2 == 1
    twist_angle = -math.pi * (time_index % half_span).astype(jnp.float32) / half_span
    difference = partner - local_part
    spectral_rhs = jnp.stack(
        [
            jnp.where(upper_half, difference * jnp.cos(twist_angle), local_part + partner),
            jnp.where(upper_half, difference * jnp.sin(twist_angle), jnp.zeros_like(local_part)),
        ]
    )
    for bit_number in range(top_bit - 1, -1, -1):
        half_span = 2**bit_number
        partner = partner_2(spectral_rhs, "tm", bit_number)
        upper_half = time_index // half_span % 2 == 1
        twist_angle = -math.pi * (time_index % half_span).astype(jnp.float32) / half_span
        twiddle = jnp.stack([jnp.cos(twist_angle), jnp.sin(twist_angle)])
        spectral_rhs = jnp.where(
            upper_half, complex_times(partner - spectral_rhs, twiddle), spectral_rhs + partner
        )
    frequency = jnp.zeros((), jnp.int32)
    for bit_number in range(section_count):
        frequency = frequency + time_index // 2**bit_number % 2 * 2 ** (
            section_count - 1 - bit_number
        )
    beta_root = alpha_wrap ** (1.0 / time_count)
    freq_angle = frequency.astype(jnp.float32) * angle_unit
    inverse_diag = inverse_of(mobility, freq_angle, beta_root)
    spectral_sol = complex_times(spectral_rhs, inverse_diag)
    for sweep_index in range(SWEEPS):
        padded_sol = extended(spectral_sol, (("space", 1),), 1)
        spectral_sol = sweep_once(padded_sol, spectral_rhs, inverse_diag, mobility)
    for bit_number in range(section_count):
        half_span = 2**bit_number
        partner = partner_2(spectral_sol, "tm", bit_number)
        upper_half = time_index // half_span % 2 == 1
        twist_angle = math.pi * (time_index % half_span).astype(jnp.float32) / half_span
        twiddle = jnp.stack([jnp.cos(twist_angle), jnp.sin(twist_angle)])
        spectral_sol = jnp.where(
            upper_half,
            partner - complex_times(spectral_sol, twiddle),
            spectral_sol + complex_times(partner, twiddle),
        )
    correction = (spectral_sol[0] / (time_count * gamma_here))[None]
    return state - correction


def ring_place(index):
    return index + index // 2 * (5 - 2 * index)


def grain_rates(labels, table_ref):
    rate = jnp.zeros(labels.shape, jnp.float32)
    for grain_id in range(GRAINS):
        rate = jnp.where(labels == grain_id, table_ref[grain_id], rate)
    return rate


def paradiag_kernel(
    slabs,
    table_ref,
    state_ref,
    initial_ref,
    labels_ref,
    out_ref,
    home,
    chunk,
    first,
    classes,
    rows_out,
    rows_in,
    planes_in,
    coupling,
    base,
    sol,
    sol_planes,
    edge_rows,
    sol_rows,
    result,
    local_sem,
    a2a_send,
    a2a_recv,
    rows_send,
    rows_recv,
    planes_send,
    planes_recv,
    sweep_send,
    sweep_recv,
    back_send,
    back_recv,
):
    t = lax.axis_index("tm")
    s = lax.axis_index("space")
    p = ring_place(t)
    below, above = lax.rem(s + slabs - 1, slabs), lax.rem(s + 1, slabs)
    depth, width = home.shape[0], home.shape[2]
    my_rows = pl.ds(pl.multiple_of(p * 8, 8), 8)

    barrier = pltpu.get_barrier_semaphore()
    for ahead in range(1, 4):
        pl.semaphore_signal(
            barrier, inc=1, device_id=(lax.rem(t + ahead, 4), s), device_id_type=MESH
        )
    for ahead in range(4):
        for slab in (below, above):
            pl.semaphore_signal(
                barrier, inc=1, device_id=(lax.rem(t + ahead, 4), slab), device_id_type=MESH
            )

    load_home = pltpu.make_async_copy(state_ref.at[0], home, local_sem.at[0])
    load_home.start()
    load_classes = pltpu.make_async_copy(labels_ref.at[:, my_rows, :], classes, local_sem.at[1])
    load_classes.start()
    load_chunk = pltpu.make_async_copy(
        state_ref.at[0, :, my_rows, :], chunk.at[t], local_sem.at[2]
    )
    load_chunk.start()
    load_first = pltpu.make_async_copy(initial_ref.at[:, my_rows, :], first, local_sem.at[3])
    load_first.start()

    load_home.wait()
    for place in range(4):
        for side, row in enumerate(((8 * place + 31) % 32, (8 * place + 8) % 32)):
            for z in range(depth):
                rows_out[place, side, z : z + 1, :] = home[z, row : row + 1, :]
    load_rows = pltpu.make_async_copy(rows_out.at[p], rows_in.at[t], local_sem.at[4])
    load_rows.start()

    pl.semaphore_wait(barrier, 11)

    sends = []
    for ahead in (2, 1, 3):
        other = lax.rem(t + ahead, 4)
        place = ring_place(other)
        other_rows = pl.ds(pl.multiple_of(place * 8, 8), 8)
        sends.append(
            pltpu.make_async_remote_copy(
                src_ref=home.at[:, other_rows, :],
                dst_ref=chunk.at[t],
                send_sem=a2a_send.at[ahead],
                recv_sem=a2a_recv.at[4 - ahead],
                device_id=(other, s),
                device_id_type=MESH,
            )
        )
        sends.append(
            pltpu.make_async_remote_copy(
                src_ref=rows_out.at[place],
                dst_ref=rows_in.at[t],
                send_sem=rows_send.at[ahead],
                recv_sem=rows_recv.at[4 - ahead],
                device_id=(other, s),
                device_id_type=MESH,
            )
        )
    for ahead in range(4):
        other = lax.rem(t + ahead, 4)
        place = ring_place(other)
        other_rows = pl.ds(pl.multiple_of(place * 8, 8), 8)
        for side, (slab, plane) in enumerate(((above, depth - 1), (below, 0))):
            sends.append(
                pltpu.make_async_remote_copy(
                    src_ref=home.at[plane, other_rows, :],
                    dst_ref=planes_in.at[t, side],
                    send_sem=planes_send.at[ahead, side],
                    recv_sem=planes_recv.at[(4 - ahead) % 4, side],
                    device_id=(other, slab),
                    device_id_type=MESH,
                )
            )
    for copy in sends:
        copy.start()

    row_number = lax.broadcasted_iota(jnp.int32, (8, width), 0)
    top, bottom = row_number == 0, row_number == 7
    beta = alpha_wrap**0.25

    load_classes.wait()
    for z in range(depth):
        rate = grain_rates(classes[z], table_ref)
        real_part = 1.0 + diag_extra * rate
        scale = 1.0 / (real_part * real_part + beta * beta)
        coupling[0, z] = 1.0 / (real_part - beta)
        coupling[1, z] = 1.0 / (real_part + beta)
        coupling[2, z] = real_part * scale
        coupling[3, z] = -beta * scale
        coupling[4, z] = rate

    load_first.wait()
    load_chunk.wait()
    load_rows.wait()
    for copy in sends:
        copy.wait_recv()

    def plane_neighbours(value, row_before, row_after):
        summed = jnp.where(top, row_before, pltpu.roll(value, 1, 0))
        summed += jnp.where(bottom, row_after, pltpu.roll(value, 7, 0))
        return summed + (pltpu.roll(value, 1, 1) + pltpu.roll(value, width - 1, 1))

    def put_edges(slot, field, z, value):
        edge_rows[slot, 0, field, z : z + 1, :] = value[7:8, :]
        edge_rows[slot, 1, field, z : z + 1, :] = value[0:1, :]

    for z in range(depth):
        rate = coupling[4, z]
        scaled = []
        for n in range(4):
            value = chunk[n, z]
            around = plane_neighbours(
                value, rows_in[n, 0, z : z + 1, :], rows_in[n, 1, z : z + 1, :]
            )
            around += chunk[n, z - 1] if z > 0 else planes_in[n, 0]
            around += chunk[n, z + 1] if z < depth - 1 else planes_in[n, 1]
            earlier = chunk[n - 1, z] if n > 0 else first[z]
            laplacian = around - 6.0 * value
            residual = (
                value
                - earlier
                + tau_step * rate * (value * value * value - value - kappa_grad * laplacian)
            )
            scaled.append(residual * alpha_wrap ** (n / 4))
        even, odd = scaled[0] + scaled[2], scaled[1] + scaled[3]
        rhs_real, rhs_imag = scaled[0] - scaled[2], scaled[3] - scaled[1]
        inv_real, inv_imag = coupling[2, z], coupling[3, z]
        starts = (
            (even + odd) * coupling[0, z],
            (even - odd) * coupling[1, z],
            rhs_real * inv_real - rhs_imag * inv_imag,
            rhs_real * inv_imag + rhs_imag * inv_real,
        )
        for field in range(4):
            base[field, z] = starts[field]
            sol[0, field, z] = starts[field]
            put_edges(0, field, z, starts[field])
            coupling[field, z] = coupling[field, z] * rate

    before, after = ring_place(lax.rem(p + 3, 4)), ring_place(lax.rem(p + 1, 4))

    def sweep_copies(j):
        copies = []
        for side, (slab, plane) in enumerate(((above, depth - 1), (below, 0))):
            copies.append(
                pltpu.make_async_remote_copy(
                    src_ref=sol.at[j, :, plane],
                    dst_ref=sol_planes.at[j, side],
                    send_sem=sweep_send.at[j, side],
                    recv_sem=sweep_recv.at[j, side],
                    device_id=(t, slab),
                    device_id_type=MESH,
                )
            )
        for side, other in enumerate((after, before)):
            copies.append(
                pltpu.make_async_remote_copy(
                    src_ref=edge_rows.at[j, side],
                    dst_ref=sol_rows.at[j, side],
                    send_sem=sweep_send.at[j, 2 + side],
                    recv_sem=sweep_recv.at[j, 2 + side],
                    device_id=(other, s),
                    device_id_type=MESH,
                )
            )
        return copies

    def sweep(j, carry):
        copies = sweep_copies(j)
        for copy in copies:
            copy.start()
        for copy in copies:
            copy.wait_recv()
        for z in range(depth):
            sums = []
            for field in range(4):
                around = plane_neighbours(
                    sol[j, field, z],
                    sol_rows[j, 0, field, z : z + 1, :],
                    sol_rows[j, 1, field, z : z + 1, :],
                )
                around += sol[j, field, z - 1] if z > 0 else sol_planes[j, 0, field]
                around += sol[j, field, z + 1] if z < depth - 1 else sol_planes[j, 1, field]
                sums.append(around)
            made = (
                base[0, z] + coupling[0, z] * sums[0],
                base[1, z] + coupling[1, z] * sums[1],
                base[2, z] + coupling[2, z] * sums[2] - coupling[3, z] * sums[3],
                base[3, z] + coupling[2, z] * sums[3] + coupling[3, z] * sums[2],
            )
            for field in range(4):
                sol[j + 1, field, z] = made[field]
                put_edges(j + 1, field, z, made[field])
        return carry

    lax.fori_loop(0, SWEEPS, sweep, 0)

    for z in range(depth):
        zero, two, real, imag = (sol[SWEEPS, field, z] for field in range(4))
        plus, minus = zero + two, zero - two
        back = (plus + 2.0 * real, minus - 2.0 * imag, plus - 2.0 * real, minus + 2.0 * imag)
        for n in range(4):
            result[n, z] = chunk[n, z] - back[n] * (0.25 * alpha_wrap ** (-n / 4))
    returns = []
    for ahead in (2, 1, 3):
        other = lax.rem(t + ahead, 4)
        returns.append(
            pltpu.make_async_remote_copy(
                src_ref=result.at[other],
                dst_ref=out_ref.at[:, my_rows, :],
                send_sem=back_send.at[ahead],
                recv_sem=back_recv.at[4 - ahead],
                device_id=(other, s),
                device_id_type=MESH,
            )
        )
    for copy in returns:
        copy.start()
    keep = pltpu.make_async_copy(result.at[t], out_ref.at[:, my_rows, :], local_sem.at[5])
    keep.start()
    for copy in sends:
        copy.wait_send()

    def drain(j, carry):
        for copy in sweep_copies(j):
            copy.wait_send()
        return carry

    lax.fori_loop(0, SWEEPS, drain, 0)
    keep.wait()
    for copy in returns:
        copy.wait()


def fused_shards(state, initial, labels, mobility_table):
    _, depth, rows, width = state.shape
    slabs = lax.axis_size("space")
    f32 = jnp.float32
    dma = pltpu.SemaphoreType.DMA
    new_state = pl.pallas_call(
        functools.partial(paradiag_kernel, slabs),
        out_shape=jax.ShapeDtypeStruct((depth, rows, width), f32),
        in_specs=[pl.BlockSpec(memory_space=pltpu.SMEM)] + [pl.BlockSpec(memory_space=pl.ANY)] * 3,
        out_specs=pl.BlockSpec(memory_space=pltpu.VMEM),
        scratch_shapes=[
            pltpu.VMEM((depth, rows, width), f32),
            pltpu.VMEM((4, depth, 8, width), f32),
            pltpu.VMEM((depth, 8, width), f32),
            pltpu.VMEM((depth, 8, width), jnp.int32),
            pltpu.VMEM((4, 2, depth, width), f32),
            pltpu.VMEM((4, 2, depth, width), f32),
            pltpu.VMEM((4, 2, 8, width), f32),
            pltpu.VMEM((5, depth, 8, width), f32),
            pltpu.VMEM((4, depth, 8, width), f32),
            pltpu.VMEM((SWEEPS + 1, 4, depth, 8, width), f32),
            pltpu.VMEM((SWEEPS, 2, 4, 8, width), f32),
            pltpu.VMEM((SWEEPS + 1, 2, 4, depth, width), f32),
            pltpu.VMEM((SWEEPS, 2, 4, depth, width), f32),
            pltpu.VMEM((4, depth, 8, width), f32),
            dma((6,)),
            dma((4,)),
            dma((4,)),
            dma((4,)),
            dma((4,)),
            dma((4, 2)),
            dma((4, 2)),
            dma((SWEEPS, 4)),
            dma((SWEEPS, 4)),
            dma((4,)),
            dma((4,)),
        ],
        compiler_params=pltpu.CompilerParams(
            collective_id=0, has_side_effects=True, vmem_limit_bytes=24 * 2**20
        ),
    )(mobility_table, state, initial, labels)
    return new_state[None]


def solution(mesh):
    in_specs = (P("tm", "space", None, None), P("space", None, None), P("space", None, None), P())
    out_specs = P("tm", "space", None, None)
    body = fused_shards if mesh.shape["tm"] == 4 and mesh.shape["space"] > 2 else shards
    return jax.shard_map(body, mesh=mesh, in_specs=in_specs, out_specs=out_specs, check_vma=False)
```

```python
import functools
import math

import jax
import jax.numpy as jnp
from jax import lax
from jax.experimental import pallas as pl
from jax.experimental.pallas import tpu as pltpu
from jax.sharding import PartitionSpec as P

MESH = pl.DeviceIdType.MESH
SWEEPS = 8
HALO = 4
BLOCKS = SWEEPS // HALO
GRAINS = 16


alpha_wrap = 0.1
tau_step = 0.25
kappa_grad = 4.0
diag_extra = 6.5


def passed_along(array, axis, by):
    devices = lax.axis_size(axis)
    pairs = [(i, i + by) for i in range(devices) if 0 <= i + by < devices]
    return lax.ppermute(array, axis, pairs)


def extended(cells, sides, width):
    for axis, dim in sides:
        count = lax.axis_size(axis)
        head = lax.slice_in_dim(cells, 0, width, axis=dim)
        tail = lax.slice_in_dim(cells, cells.shape[dim] - width, cells.shape[dim], axis=dim)
        cells = jnp.concatenate(
            [
                lax.ppermute(tail, axis, [(i, (i + 1) % count) for i in range(count)]),
                cells,
                lax.ppermute(head, axis, [((i + 1) % count, i) for i in range(count)]),
            ],
            axis=dim,
        )
    return cells


def partner_2(value, axis, apart):
    mask = 2**apart
    pairs = [(source, source ^ mask) for source in range(lax.axis_size(axis))]
    return lax.ppermute(value, axis, pairs)


def plane_sum(grid_field):
    summed = jnp.roll(grid_field, 1, -2) + jnp.roll(grid_field, -1, -2)
    return summed + jnp.roll(grid_field, 1, -1) + jnp.roll(grid_field, -1, -1)


def mobility_of(labels, rate_table):

    def add_grain(grain_id, summed):
        return summed + jnp.where(
            labels == grain_id, rate_table[grain_id], jnp.zeros((), rate_table.dtype)
        )

    return lax.fori_loop(0, GRAINS, add_grain, jnp.zeros(labels.shape, rate_table.dtype))


def complex_times(left_val, right_val):
    return jnp.stack(
        [
            left_val[0] * right_val[0] - left_val[1] * right_val[1],
            left_val[0] * right_val[1] + left_val[1] * right_val[0],
        ]
    )


def sweep_once(padded, spectral_rhs, inverse_diag, mobility):
    middle = padded[:, 1:-1]
    summed = spectral_rhs + mobility * (padded[:, 2:] + padded[:, :-2] + plane_sum(middle))
    return complex_times(summed, inverse_diag)


def inverse_of(mobility, freq_angle, beta_root):
    diag_real = 1.0 - beta_root * jnp.cos(freq_angle) + diag_extra * mobility
    diag_imag = beta_root * jnp.sin(freq_angle)
    magnitude = diag_real * diag_real + diag_imag * diag_imag
    return jnp.stack([diag_real / magnitude, -diag_imag / magnitude])


def shards(state, initial, labels, mobility_table):
    time_count = lax.axis_size("tm")
    section_count = time_count.bit_length() - 1
    time_index = lax.axis_index("tm")
    index_float = time_index.astype(jnp.float32)
    angle_unit = 2.0 * math.pi / time_count
    gamma_here = alpha_wrap ** (index_float / time_count)
    current = state[0]
    mobility = mobility_of(labels, mobility_table)
    earlier = passed_along(state, "tm", 1)
    earlier_step = jnp.where(time_index == 0, initial, earlier[0])
    padded = extended(current, (("space", 0),), 1)
    laplacian = padded[2:] + padded[:-2] + plane_sum(current) - 6.0 * current
    residual = (
        current
        - earlier_step
        + tau_step * mobility * (current * current * current - current - kappa_grad * laplacian)
    )
    top_bit = section_count - 1
    half_span = 2**top_bit
    local_part = residual * gamma_here
    partner = partner_2(local_part, "tm", top_bit)
    upper_half = time_index // half_span % 2 == 1
    twist_angle = -math.pi * (time_index % half_span).astype(jnp.float32) / half_span
    difference = partner - local_part
    spectral_rhs = jnp.stack(
        [
            jnp.where(upper_half, difference * jnp.cos(twist_angle), local_part + partner),
            jnp.where(upper_half, difference * jnp.sin(twist_angle), jnp.zeros_like(local_part)),
        ]
    )
    for bit_number in range(top_bit - 1, -1, -1):
        half_span = 2**bit_number
        partner = partner_2(spectral_rhs, "tm", bit_number)
        upper_half = time_index // half_span % 2 == 1
        twist_angle = -math.pi * (time_index % half_span).astype(jnp.float32) / half_span
        twiddle = jnp.stack([jnp.cos(twist_angle), jnp.sin(twist_angle)])
        spectral_rhs = jnp.where(
            upper_half, complex_times(partner - spectral_rhs, twiddle), spectral_rhs + partner
        )
    frequency = jnp.zeros((), jnp.int32)
    for bit_number in range(section_count):
        frequency = frequency + time_index // 2**bit_number % 2 * 2 ** (
            section_count - 1 - bit_number
        )
    beta_root = alpha_wrap ** (1.0 / time_count)
    freq_angle = frequency.astype(jnp.float32) * angle_unit
    inverse_diag = inverse_of(mobility, freq_angle, beta_root)
    spectral_sol = complex_times(spectral_rhs, inverse_diag)
    for sweep_index in range(SWEEPS):
        padded_sol = extended(spectral_sol, (("space", 1),), 1)
        spectral_sol = sweep_once(padded_sol, spectral_rhs, inverse_diag, mobility)
    for bit_number in range(section_count):
        half_span = 2**bit_number
        partner = partner_2(spectral_sol, "tm", bit_number)
        upper_half = time_index // half_span % 2 == 1
        twist_angle = math.pi * (time_index % half_span).astype(jnp.float32) / half_span
        twiddle = jnp.stack([jnp.cos(twist_angle), jnp.sin(twist_angle)])
        spectral_sol = jnp.where(
            upper_half,
            partner - complex_times(spectral_sol, twiddle),
            spectral_sol + complex_times(partner, twiddle),
        )
    correction = (spectral_sol[0] / (time_count * gamma_here))[None]
    return state - correction


def ring_place(index):
    return index + index // 2 * (5 - 2 * index)


def grain_rates(labels, table_ref):
    rate = jnp.zeros(labels.shape, jnp.float32)
    for grain_id in range(GRAINS):
        rate = jnp.where(labels == grain_id, table_ref[grain_id], rate)
    return rate


def paradiag_kernel(
    slabs,
    table_ref,
    state_ref,
    initial_ref,
    labels_ref,
    out_ref,
    home,
    chunk,
    first,
    classes,
    rows_out,
    rows_in,
    planes_in,
    coupling,
    box_coupling,
    base,
    sol,
    own,
    own_in,
    edges,
    edges_in,
    result,
    local_sem,
    a2a_send,
    a2a_recv,
    rows_send,
    rows_recv,
    planes_send,
    planes_recv,
    class_send,
    class_recv,
    halo_send,
    halo_recv,
    back_send,
    back_recv,
):
    t = lax.axis_index("tm")
    s = lax.axis_index("space")
    p = ring_place(t)
    below, above = lax.rem(s + slabs - 1, slabs), lax.rem(s + 1, slabs)
    depth, width = home.shape[0], home.shape[2]
    my_rows = pl.ds(pl.multiple_of(p * 8, 8), 8)

    barrier = pltpu.get_barrier_semaphore()
    for ahead in range(1, 4):
        pl.semaphore_signal(
            barrier, inc=1, device_id=(lax.rem(t + ahead, 4), s), device_id_type=MESH
        )
    for ahead in range(4):
        for slab in (below, above):
            pl.semaphore_signal(
                barrier, inc=1, device_id=(lax.rem(t + ahead, 4), slab), device_id_type=MESH
            )

    load_home = pltpu.make_async_copy(state_ref.at[0], home, local_sem.at[0])
    load_home.start()
    chunk_rows = [
        pl.ds(pl.multiple_of(lax.rem(p + shift, 4) * 8, 8), 8) for shift in (3, 0, 1)
    ]
    load_classes = [
        pltpu.make_async_copy(
            labels_ref.at[:, chunk_rows[side], :],
            classes.at[pl.ds(HALO, depth), side],
            local_sem.at[6 + side],
        )
        for side in range(3)
    ]
    for copy in load_classes:
        copy.start()
    load_chunk = pltpu.make_async_copy(
        state_ref.at[0, :, my_rows, :], chunk.at[t], local_sem.at[2]
    )
    load_chunk.start()
    load_first = pltpu.make_async_copy(initial_ref.at[:, my_rows, :], first, local_sem.at[3])
    load_first.start()

    load_home.wait()
    for place in range(4):
        for side, row in enumerate(((8 * place + 31) % 32, (8 * place + 8) % 32)):
            for z in range(depth):
                rows_out[place, side, z : z + 1, :] = home[z, row : row + 1, :]
    load_rows = pltpu.make_async_copy(rows_out.at[p], rows_in.at[t], local_sem.at[4])
    load_rows.start()

    pl.semaphore_wait(barrier, 11)

    sends = []
    for ahead in (2, 1, 3):
        other = lax.rem(t + ahead, 4)
        place = ring_place(other)
        other_rows = pl.ds(pl.multiple_of(place * 8, 8), 8)
        sends.append(
            pltpu.make_async_remote_copy(
                src_ref=home.at[:, other_rows, :],
                dst_ref=chunk.at[t],
                send_sem=a2a_send.at[ahead],
                recv_sem=a2a_recv.at[4 - ahead],
                device_id=(other, s),
                device_id_type=MESH,
            )
        )
        sends.append(
            pltpu.make_async_remote_copy(
                src_ref=rows_out.at[place],
                dst_ref=rows_in.at[t],
                send_sem=rows_send.at[ahead],
                recv_sem=rows_recv.at[4 - ahead],
                device_id=(other, s),
                device_id_type=MESH,
            )
        )
    for ahead in range(4):
        other = lax.rem(t + ahead, 4)
        place = ring_place(other)
        other_rows = pl.ds(pl.multiple_of(place * 8, 8), 8)
        for side, (slab, plane) in enumerate(((above, depth - 1), (below, 0))):
            sends.append(
                pltpu.make_async_remote_copy(
                    src_ref=home.at[plane, other_rows, :],
                    dst_ref=planes_in.at[t, side],
                    send_sem=planes_send.at[ahead, side],
                    recv_sem=planes_recv.at[(4 - ahead) % 4, side],
                    device_id=(other, slab),
                    device_id_type=MESH,
                )
            )
    class_sends = []
    for side in range(3):
        for way, (slab, start, place) in enumerate(
            ((above, depth - HALO, 0), (below, 0, HALO + depth))
        ):
            class_sends.append(
                pltpu.make_async_remote_copy(
                    src_ref=labels_ref.at[pl.ds(start, HALO), chunk_rows[side], :],
                    dst_ref=classes.at[pl.ds(place, HALO), side],
                    send_sem=class_send.at[side, way],
                    recv_sem=class_recv.at[side, way],
                    device_id=(t, slab),
                    device_id_type=MESH,
                )
            )
    for copy in sends + class_sends:
        copy.start()

    row_number = lax.broadcasted_iota(jnp.int32, (8, width), 0)
    top, bottom = row_number == 0, row_number == 7
    upper = row_number < 4
    beta = alpha_wrap**0.25

    for copy in load_classes:
        copy.wait()
    for z in range(depth):
        rate = grain_rates(classes[HALO + z, 1], table_ref)
        real_part = 1.0 + diag_extra * rate
        scale = 1.0 / (real_part * real_part + beta * beta)
        coupling[0, z] = 1.0 / (real_part - beta)
        coupling[1, z] = 1.0 / (real_part + beta)
        coupling[2, z] = real_part * scale
        coupling[3, z] = -beta * scale
        coupling[4, z] = rate

    for copy in class_sends:
        copy.wait_recv()

    def swap(value):
        return pltpu.roll(value, 4, 0)

    def box_plane(z, carry):
        middle = swap(classes[z, 1])
        for part, label in enumerate(
            (
                jnp.where(upper, swap(classes[z, 0]), middle),
                jnp.where(upper, middle, swap(classes[z, 2])),
            )
        ):
            rate = grain_rates(label, table_ref)
            real_part = 1.0 + diag_extra * rate
            scale = rate / (real_part * real_part + beta * beta)
            rows = slice(8 * part, 8 * part + 8)
            box_coupling[0, z, rows] = rate / (real_part - beta)
            box_coupling[1, z, rows] = rate / (real_part + beta)
            box_coupling[2, z, rows] = real_part * scale
            box_coupling[3, z, rows] = beta * scale
        return carry

    lax.fori_loop(0, depth + 2 * HALO, box_plane, 0)

    load_first.wait()
    load_chunk.wait()
    load_rows.wait()
    for copy in sends:
        copy.wait_recv()

    def plane_neighbours(value, row_before, row_after):
        summed = jnp.where(top, row_before, pltpu.roll(value, 1, 0))
        summed += jnp.where(bottom, row_after, pltpu.roll(value, 7, 0))
        return summed + (pltpu.roll(value, 1, 1) + pltpu.roll(value, width - 1, 1))

    for z in range(depth):
        rate = coupling[4, z]
        scaled = []
        for n in range(4):
            value = chunk[n, z]
            around = plane_neighbours(
                value, rows_in[n, 0, z : z + 1, :], rows_in[n, 1, z : z + 1, :]
            )
            around += chunk[n, z - 1] if z > 0 else planes_in[n, 0]
            around += chunk[n, z + 1] if z < depth - 1 else planes_in[n, 1]
            earlier = chunk[n - 1, z] if n > 0 else first[z]
            laplacian = around - 6.0 * value
            residual = (
                value
                - earlier
                + tau_step * rate * (value * value * value - value - kappa_grad * laplacian)
            )
            scaled.append(residual * alpha_wrap ** (n / 4))
        even, odd = scaled[0] + scaled[2], scaled[1] + scaled[3]
        rhs_real, rhs_imag = scaled[0] - scaled[2], scaled[3] - scaled[1]
        inv_real, inv_imag = coupling[2, z], coupling[3, z]
        starts = (
            (even + odd) * coupling[0, z],
            (even - odd) * coupling[1, z],
            rhs_real * inv_real - rhs_imag * inv_imag,
            rhs_real * inv_imag + rhs_imag * inv_real,
        )
        for field in range(4):
            own[0, field, z] = starts[field]

    before, after = ring_place(lax.rem(p + 3, 4)), ring_place(lax.rem(p + 1, 4))

    def block_copies(block):
        moves = []
        for side, (slab, start) in enumerate(((above, depth - HALO), (below, 0))):
            moves.append(
                (own.at[block, :, pl.ds(start, HALO)], own_in.at[block, side], (t, slab))
            )
        for side, other in enumerate((after, before)):
            moves.append(
                (edges.at[block, side], edges_in.at[block, side, pl.ds(1, 2)], (other, s))
            )
            for slab, half, place in ((above, 1, 0), (below, 0, 3)):
                moves.append(
                    (
                        edges.at[block, side, half],
                        edges_in.at[block, side, place],
                        (other, slab),
                    )
                )
        return [
            pltpu.make_async_remote_copy(
                src_ref=source,
                dst_ref=target,
                send_sem=halo_send.at[block, number],
                recv_sem=halo_recv.at[block, number],
                device_id=device,
                device_id_type=MESH,
            )
            for number, (source, target, device) in enumerate(moves)
        ]

    def put_edges(block):
        def of_field(field, carry):
            for half in range(2):
                for i in range(2):
                    one = own[block, field, 4 * half + i]
                    two = own[block, field, 4 * half + i + 2]
                    edges[block, 0, half, field, i] = jnp.where(upper, swap(one), two)
                    edges[block, 1, half, field, i] = jnp.where(upper, one, swap(two))
            return carry

        lax.fori_loop(0, 4, of_field, 0)

    def assemble(block, target):
        def of_field(field, carry):
            for z in range(depth + 2 * HALO):
                quarter, late, i = z // 4, z % 4 // 2, z % 2
                if quarter == 0:
                    middle = own_in[block, 0, field, z]
                elif quarter == 3:
                    middle = own_in[block, 1, field, z - HALO - depth]
                else:
                    middle = own[block, field, z - HALO]
                middle = swap(middle)
                low = edges_in[block, 0, quarter, field, i]
                high = edges_in[block, 1, quarter, field, i]
                low = swap(low) if late else low
                high = high if late else swap(high)
                target[field, z, 0:8] = jnp.where(upper, low, middle)
                target[field, z, 8:16] = jnp.where(upper, middle, high)
            return carry

        lax.fori_loop(0, 4, of_field, 0)

    def sweep(source, target, first_plane, last_plane):
        def two_planes(pair, carry):
            for extra in range(2):
                z = first_plane + 2 * pair + extra
                sums = []
                for field in range(4):
                    value = source[field, z]
                    around = pltpu.roll(value, 1, 0) + pltpu.roll(value, 15, 0)
                    around += pltpu.roll(value, 1, 1) + pltpu.roll(value, width - 1, 1)
                    sums.append(around + (source[field, z - 1] + source[field, z + 1]))
                real, imag = box_coupling[2, z], box_coupling[3, z]
                target[0, z] = base[0, z] + box_coupling[0, z] * sums[0]
                target[1, z] = base[1, z] + box_coupling[1, z] * sums[1]
                target[2, z] = base[2, z] + real * sums[2] + imag * sums[3]
                target[3, z] = base[3, z] + real * sums[3] - imag * sums[2]
            return carry

        lax.fori_loop(0, (last_plane - first_plane) // 2, two_planes, 0)

    halos = []
    for block in range(BLOCKS):
        put_edges(block)
        copies = block_copies(block)
        halos += copies
        for copy in copies:
            copy.start()
        for copy in copies:
            copy.wait_recv()
        source = base if block == 0 else sol.at[0]
        assemble(block, source)
        for step in range(HALO):
            target = sol.at[(step + 1) % 2]
            sweep(source, target, step + 1, depth + 2 * HALO - 1 - step)
            source = target

        def take_own(field, carry):
            for z in range(depth):
                own[block + 1, field, z] = jnp.where(
                    upper,
                    swap(sol[0, field, HALO + z, 0:8]),
                    swap(sol[0, field, HALO + z, 8:16]),
                )
            return carry

        lax.fori_loop(0, 4, take_own, 0)

    for z in range(depth):
        zero, two, real, imag = (own[BLOCKS, field, z] for field in range(4))
        plus, minus = zero + two, zero - two
        back = (plus + 2.0 * real, minus - 2.0 * imag, plus - 2.0 * real, minus + 2.0 * imag)
        for n in range(4):
            result[n, z] = chunk[n, z] - back[n] * (0.25 * alpha_wrap ** (-n / 4))
    returns = []
    for ahead in (2, 1, 3):
        other = lax.rem(t + ahead, 4)
        returns.append(
            pltpu.make_async_remote_copy(
                src_ref=result.at[other],
                dst_ref=out_ref.at[:, my_rows, :],
                send_sem=back_send.at[ahead],
                recv_sem=back_recv.at[4 - ahead],
                device_id=(other, s),
                device_id_type=MESH,
            )
        )
    for copy in returns:
        copy.start()
    keep = pltpu.make_async_copy(result.at[t], out_ref.at[:, my_rows, :], local_sem.at[5])
    keep.start()
    for copy in sends + class_sends + halos:
        copy.wait_send()
    keep.wait()
    for copy in returns:
        copy.wait()


def fused_shards(state, initial, labels, mobility_table):
    _, depth, rows, width = state.shape
    slabs = lax.axis_size("space")
    f32 = jnp.float32
    dma = pltpu.SemaphoreType.DMA
    new_state = pl.pallas_call(
        functools.partial(paradiag_kernel, slabs),
        out_shape=jax.ShapeDtypeStruct((depth, rows, width), f32),
        in_specs=[pl.BlockSpec(memory_space=pltpu.SMEM)] + [pl.BlockSpec(memory_space=pl.ANY)] * 3,
        out_specs=pl.BlockSpec(memory_space=pltpu.VMEM),
        scratch_shapes=[
            pltpu.VMEM((depth, rows, width), f32),
            pltpu.VMEM((4, depth, 8, width), f32),
            pltpu.VMEM((depth, 8, width), f32),
            pltpu.VMEM((depth + 2 * HALO, 3, 8, width), jnp.int32),
            pltpu.VMEM((4, 2, depth, width), f32),
            pltpu.VMEM((4, 2, depth, width), f32),
            pltpu.VMEM((4, 2, 8, width), f32),
            pltpu.VMEM((5, depth, 8, width), f32),
            pltpu.VMEM((4, depth + 2 * HALO, 16, width), f32),
            pltpu.VMEM((4, depth + 2 * HALO, 16, width), f32),
            pltpu.VMEM((2, 4, depth + 2 * HALO, 16, width), f32),
            pltpu.VMEM((BLOCKS + 1, 4, depth, 8, width), f32),
            pltpu.VMEM((BLOCKS, 2, 4, HALO, 8, width), f32),
            pltpu.VMEM((BLOCKS, 2, 2, 4, 2, 8, width), f32),
            pltpu.VMEM((BLOCKS, 2, 4, 4, 2, 8, width), f32),
            pltpu.VMEM((4, depth, 8, width), f32),
            dma((9,)),
            dma((4,)),
            dma((4,)),
            dma((4,)),
            dma((4,)),
            dma((4, 2)),
            dma((4, 2)),
            dma((3, 2)),
            dma((3, 2)),
            dma((BLOCKS, 8)),
            dma((BLOCKS, 8)),
            dma((4,)),
            dma((4,)),
        ],
        compiler_params=pltpu.CompilerParams(
            collective_id=0, has_side_effects=True, vmem_limit_bytes=40 * 2**20
        ),
    )(mobility_table, state, initial, labels)
    return new_state[None]


def solution(mesh):
    in_specs = (P("tm", "space", None, None), P("space", None, None), P("space", None, None), P())
    out_specs = P("tm", "space", None, None)
    body = fused_shards if mesh.shape["tm"] == 4 and mesh.shape["space"] > 2 else shards
    return jax.shard_map(body, mesh=mesh, in_specs=in_specs, out_specs=out_specs, check_vma=False)
```

```python
import functools
import math

import jax
import jax.numpy as jnp
from jax import lax
from jax.experimental import pallas as pl
from jax.experimental.pallas import tpu as pltpu
from jax.sharding import PartitionSpec as P

MESH = pl.DeviceIdType.MESH
SWEEPS = 8
HALO = 4
BLOCKS = SWEEPS // HALO
GRAINS = 16


alpha_wrap = 0.1
tau_step = 0.25
kappa_grad = 4.0
diag_extra = 6.5


def passed_along(array, axis, by):
    devices = lax.axis_size(axis)
    pairs = [(i, i + by) for i in range(devices) if 0 <= i + by < devices]
    return lax.ppermute(array, axis, pairs)


def extended(cells, sides, width):
    for axis, dim in sides:
        count = lax.axis_size(axis)
        head = lax.slice_in_dim(cells, 0, width, axis=dim)
        tail = lax.slice_in_dim(cells, cells.shape[dim] - width, cells.shape[dim], axis=dim)
        cells = jnp.concatenate(
            [
                lax.ppermute(tail, axis, [(i, (i + 1) % count) for i in range(count)]),
                cells,
                lax.ppermute(head, axis, [((i + 1) % count, i) for i in range(count)]),
            ],
            axis=dim,
        )
    return cells


def partner_2(value, axis, apart):
    mask = 2**apart
    pairs = [(source, source ^ mask) for source in range(lax.axis_size(axis))]
    return lax.ppermute(value, axis, pairs)


def plane_sum(grid_field):
    summed = jnp.roll(grid_field, 1, -2) + jnp.roll(grid_field, -1, -2)
    return summed + jnp.roll(grid_field, 1, -1) + jnp.roll(grid_field, -1, -1)


def mobility_of(labels, rate_table):

    def add_grain(grain_id, summed):
        return summed + jnp.where(
            labels == grain_id, rate_table[grain_id], jnp.zeros((), rate_table.dtype)
        )

    return lax.fori_loop(0, GRAINS, add_grain, jnp.zeros(labels.shape, rate_table.dtype))


def complex_times(left_val, right_val):
    return jnp.stack(
        [
            left_val[0] * right_val[0] - left_val[1] * right_val[1],
            left_val[0] * right_val[1] + left_val[1] * right_val[0],
        ]
    )


def sweep_once(padded, spectral_rhs, inverse_diag, mobility):
    middle = padded[:, 1:-1]
    summed = spectral_rhs + mobility * (padded[:, 2:] + padded[:, :-2] + plane_sum(middle))
    return complex_times(summed, inverse_diag)


def inverse_of(mobility, freq_angle, beta_root):
    diag_real = 1.0 - beta_root * jnp.cos(freq_angle) + diag_extra * mobility
    diag_imag = beta_root * jnp.sin(freq_angle)
    magnitude = diag_real * diag_real + diag_imag * diag_imag
    return jnp.stack([diag_real / magnitude, -diag_imag / magnitude])


def shards(state, initial, labels, mobility_table):
    time_count = lax.axis_size("tm")
    section_count = time_count.bit_length() - 1
    time_index = lax.axis_index("tm")
    index_float = time_index.astype(jnp.float32)
    angle_unit = 2.0 * math.pi / time_count
    gamma_here = alpha_wrap ** (index_float / time_count)
    current = state[0]
    mobility = mobility_of(labels, mobility_table)
    earlier = passed_along(state, "tm", 1)
    earlier_step = jnp.where(time_index == 0, initial, earlier[0])
    padded = extended(current, (("space", 0),), 1)
    laplacian = padded[2:] + padded[:-2] + plane_sum(current) - 6.0 * current
    residual = (
        current
        - earlier_step
        + tau_step * mobility * (current * current * current - current - kappa_grad * laplacian)
    )
    top_bit = section_count - 1
    half_span = 2**top_bit
    local_part = residual * gamma_here
    partner = partner_2(local_part, "tm", top_bit)
    upper_half = time_index // half_span % 2 == 1
    twist_angle = -math.pi * (time_index % half_span).astype(jnp.float32) / half_span
    difference = partner - local_part
    spectral_rhs = jnp.stack(
        [
            jnp.where(upper_half, difference * jnp.cos(twist_angle), local_part + partner),
            jnp.where(upper_half, difference * jnp.sin(twist_angle), jnp.zeros_like(local_part)),
        ]
    )
    for bit_number in range(top_bit - 1, -1, -1):
        half_span = 2**bit_number
        partner = partner_2(spectral_rhs, "tm", bit_number)
        upper_half = time_index // half_span % 2 == 1
        twist_angle = -math.pi * (time_index % half_span).astype(jnp.float32) / half_span
        twiddle = jnp.stack([jnp.cos(twist_angle), jnp.sin(twist_angle)])
        spectral_rhs = jnp.where(
            upper_half, complex_times(partner - spectral_rhs, twiddle), spectral_rhs + partner
        )
    frequency = jnp.zeros((), jnp.int32)
    for bit_number in range(section_count):
        frequency = frequency + time_index // 2**bit_number % 2 * 2 ** (
            section_count - 1 - bit_number
        )
    beta_root = alpha_wrap ** (1.0 / time_count)
    freq_angle = frequency.astype(jnp.float32) * angle_unit
    inverse_diag = inverse_of(mobility, freq_angle, beta_root)
    spectral_sol = complex_times(spectral_rhs, inverse_diag)
    for sweep_index in range(SWEEPS):
        padded_sol = extended(spectral_sol, (("space", 1),), 1)
        spectral_sol = sweep_once(padded_sol, spectral_rhs, inverse_diag, mobility)
    for bit_number in range(section_count):
        half_span = 2**bit_number
        partner = partner_2(spectral_sol, "tm", bit_number)
        upper_half = time_index // half_span % 2 == 1
        twist_angle = math.pi * (time_index % half_span).astype(jnp.float32) / half_span
        twiddle = jnp.stack([jnp.cos(twist_angle), jnp.sin(twist_angle)])
        spectral_sol = jnp.where(
            upper_half,
            partner - complex_times(spectral_sol, twiddle),
            spectral_sol + complex_times(partner, twiddle),
        )
    correction = (spectral_sol[0] / (time_count * gamma_here))[None]
    return state - correction


def ring_place(index):
    return index + index // 2 * (5 - 2 * index)


def grain_rates(labels, table_ref):
    rate = jnp.zeros(labels.shape, jnp.float32)
    for grain_id in range(GRAINS):
        rate = jnp.where(labels == grain_id, table_ref[grain_id], rate)
    return rate


def paradiag_kernel(
    slabs,
    table_ref,
    state_ref,
    initial_ref,
    labels_ref,
    out_ref,
    home,
    chunk,
    first,
    classes,
    rows_out,
    rows_in,
    planes_in,
    coupling,
    box_coupling,
    base,
    sol,
    own,
    own_in,
    edges,
    edges_in,
    corners,
    corners_in,
    result,
    local_sem,
    a2a_send,
    a2a_recv,
    rows_send,
    rows_recv,
    planes_send,
    planes_recv,
    class_send,
    class_recv,
    halo_send,
    halo_recv,
    back_send,
    back_recv,
):
    t = lax.axis_index("tm")
    s = lax.axis_index("space")
    p = ring_place(t)
    below, above = lax.rem(s + slabs - 1, slabs), lax.rem(s + 1, slabs)
    depth, width = home.shape[0], home.shape[2]
    my_rows = pl.ds(pl.multiple_of(p * 8, 8), 8)

    barrier = pltpu.get_barrier_semaphore()
    for ahead in range(1, 4):
        pl.semaphore_signal(
            barrier, inc=1, device_id=(lax.rem(t + ahead, 4), s), device_id_type=MESH
        )
    for ahead in range(4):
        for slab in (below, above):
            pl.semaphore_signal(
                barrier, inc=1, device_id=(lax.rem(t + ahead, 4), slab), device_id_type=MESH
            )

    load_home = pltpu.make_async_copy(state_ref.at[0], home, local_sem.at[0])
    load_home.start()
    chunk_rows = [
        pl.ds(pl.multiple_of(lax.rem(p + shift, 4) * 8, 8), 8) for shift in (3, 0, 1)
    ]
    load_classes = [
        pltpu.make_async_copy(
            labels_ref.at[:, chunk_rows[side], :],
            classes.at[pl.ds(HALO, depth), side],
            local_sem.at[6 + side],
        )
        for side in range(3)
    ]
    for copy in load_classes:
        copy.start()
    load_chunk = pltpu.make_async_copy(
        state_ref.at[0, :, my_rows, :], chunk.at[t], local_sem.at[2]
    )
    load_chunk.start()
    load_first = pltpu.make_async_copy(initial_ref.at[:, my_rows, :], first, local_sem.at[3])
    load_first.start()

    load_home.wait()
    for place in range(4):
        for side, row in enumerate(((8 * place + 31) % 32, (8 * place + 8) % 32)):
            for z in range(depth):
                rows_out[place, side, z : z + 1, :] = home[z, row : row + 1, :]
    load_rows = pltpu.make_async_copy(rows_out.at[p], rows_in.at[t], local_sem.at[4])
    load_rows.start()

    pl.semaphore_wait(barrier, 11)

    sends = []
    for ahead in (2, 1, 3):
        other = lax.rem(t + ahead, 4)
        place = ring_place(other)
        other_rows = pl.ds(pl.multiple_of(place * 8, 8), 8)
        sends.append(
            pltpu.make_async_remote_copy(
                src_ref=home.at[:, other_rows, :],
                dst_ref=chunk.at[t],
                send_sem=a2a_send.at[ahead],
                recv_sem=a2a_recv.at[4 - ahead],
                device_id=(other, s),
                device_id_type=MESH,
            )
        )
        sends.append(
            pltpu.make_async_remote_copy(
                src_ref=rows_out.at[place],
                dst_ref=rows_in.at[t],
                send_sem=rows_send.at[ahead],
                recv_sem=rows_recv.at[4 - ahead],
                device_id=(other, s),
                device_id_type=MESH,
            )
        )
    for ahead in range(4):
        other = lax.rem(t + ahead, 4)
        place = ring_place(other)
        other_rows = pl.ds(pl.multiple_of(place * 8, 8), 8)
        for side, (slab, plane) in enumerate(((above, depth - 1), (below, 0))):
            sends.append(
                pltpu.make_async_remote_copy(
                    src_ref=home.at[plane, other_rows, :],
                    dst_ref=planes_in.at[t, side],
                    send_sem=planes_send.at[ahead, side],
                    recv_sem=planes_recv.at[(4 - ahead) % 4, side],
                    device_id=(other, slab),
                    device_id_type=MESH,
                )
            )
    class_sends = []
    for side in range(3):
        for way, (slab, start, place) in enumerate(
            ((above, depth - HALO, 0), (below, 0, HALO + depth))
        ):
            class_sends.append(
                pltpu.make_async_remote_copy(
                    src_ref=labels_ref.at[pl.ds(start, HALO), chunk_rows[side], :],
                    dst_ref=classes.at[pl.ds(place, HALO), side],
                    send_sem=class_send.at[side, way],
                    recv_sem=class_recv.at[side, way],
                    device_id=(t, slab),
                    device_id_type=MESH,
                )
            )
    for copy in sends + class_sends:
        copy.start()

    row_number = lax.broadcasted_iota(jnp.int32, (8, width), 0)
    top, bottom = row_number == 0, row_number == 7
    upper = row_number < 4
    beta = alpha_wrap**0.25

    for copy in load_classes:
        copy.wait()
    for z in range(depth):
        rate = grain_rates(classes[HALO + z, 1], table_ref)
        real_part = 1.0 + diag_extra * rate
        scale = 1.0 / (real_part * real_part + beta * beta)
        coupling[0, z] = 1.0 / (real_part - beta)
        coupling[1, z] = 1.0 / (real_part + beta)
        coupling[2, z] = real_part * scale
        coupling[3, z] = -beta * scale
        coupling[4, z] = rate

    for copy in class_sends:
        copy.wait_recv()

    def swap(value):
        return pltpu.roll(value, 4, 0)

    def box_plane(z, carry):
        middle = swap(classes[z, 1])
        for part, label in enumerate(
            (
                jnp.where(upper, swap(classes[z, 0]), middle),
                jnp.where(upper, middle, swap(classes[z, 2])),
            )
        ):
            rate = grain_rates(label, table_ref)
            real_part = 1.0 + diag_extra * rate
            scale = rate / (real_part * real_part + beta * beta)
            rows = slice(8 * part, 8 * part + 8)
            box_coupling[0, z, rows] = rate / (real_part - beta)
            box_coupling[1, z, rows] = rate / (real_part + beta)
            box_coupling[2, z, rows] = real_part * scale
            box_coupling[3, z, rows] = beta * scale
        return carry

    lax.fori_loop(0, depth + 2 * HALO, box_plane, 0)

    load_first.wait()
    load_chunk.wait()
    load_rows.wait()
    for copy in sends:
        copy.wait_recv()

    def plane_neighbours(value, row_before, row_after):
        summed = jnp.where(top, row_before, pltpu.roll(value, 1, 0))
        summed += jnp.where(bottom, row_after, pltpu.roll(value, 7, 0))
        return summed + (pltpu.roll(value, 1, 1) + pltpu.roll(value, width - 1, 1))

    for z in range(depth):
        rate = coupling[4, z]
        scaled = []
        for n in range(4):
            value = chunk[n, z]
            around = plane_neighbours(
                value, rows_in[n, 0, z : z + 1, :], rows_in[n, 1, z : z + 1, :]
            )
            around += chunk[n, z - 1] if z > 0 else planes_in[n, 0]
            around += chunk[n, z + 1] if z < depth - 1 else planes_in[n, 1]
            earlier = chunk[n - 1, z] if n > 0 else first[z]
            laplacian = around - 6.0 * value
            residual = (
                value
                - earlier
                + tau_step * rate * (value * value * value - value - kappa_grad * laplacian)
            )
            scaled.append(residual * alpha_wrap ** (n / 4))
        even, odd = scaled[0] + scaled[2], scaled[1] + scaled[3]
        rhs_real, rhs_imag = scaled[0] - scaled[2], scaled[3] - scaled[1]
        inv_real, inv_imag = coupling[2, z], coupling[3, z]
        starts = (
            (even + odd) * coupling[0, z],
            (even - odd) * coupling[1, z],
            rhs_real * inv_real - rhs_imag * inv_imag,
            rhs_real * inv_imag + rhs_imag * inv_real,
        )
        for field in range(4):
            own[0, field, z] = starts[field]

    before, after = ring_place(lax.rem(p + 3, 4)), ring_place(lax.rem(p + 1, 4))

    def block_copies(block):
        moves = []
        for side, (slab, start) in enumerate(((above, depth - HALO), (below, 0))):
            moves.append(
                (own.at[block, :, pl.ds(start, HALO)], own_in.at[block, side], (t, slab))
            )
        for side, other in enumerate((after, before)):
            moves.append(
                (edges.at[block, side], edges_in.at[block, side], (other, s))
            )
            for slab, half, place in ((above, 1, 0), (below, 0, 1)):
                moves.append(
                    (
                        corners.at[block, side, half],
                        corners_in.at[block, side, place],
                        (other, slab),
                    )
                )
        return [
            pltpu.make_async_remote_copy(
                src_ref=source,
                dst_ref=target,
                send_sem=halo_send.at[block, number],
                recv_sem=halo_recv.at[block, number],
                device_id=device,
                device_id_type=MESH,
            )
            for number, (source, target, device) in enumerate(moves)
        ]

    def put_edges(block):
        def of_field(field, carry):
            for half in range(2):
                for i in range(2):
                    one = own[block, field, 4 * half + i]
                    two = own[block, field, 4 * half + i + 2]
                    edges[block, 0, half, field, i] = jnp.where(upper, swap(one), two)
                    edges[block, 1, half, field, i] = jnp.where(upper, one, swap(two))
            for half, nearest in enumerate(((0, 1, 2), (depth - 1, depth - 2, depth - 3))):
                one, two, three = (own[block, field, z] for z in nearest)
                two_three = jnp.where(row_number == 5, pltpu.roll(three, 6, 0), two)
                corners[block, 0, half, field] = jnp.where(upper, swap(one), two_three)
                two_three = jnp.where(row_number == 2, pltpu.roll(three, 2, 0), two)
                corners[block, 1, half, field] = jnp.where(upper, two_three, swap(one))
            return carry

        lax.fori_loop(0, 4, of_field, 0)

    def assemble(block, target):
        def of_field(field, carry):
            for z in range(depth + 2 * HALO):
                quarter, late, i = z // 4, z % 4 // 2, z % 2
                if quarter == 0:
                    middle = own_in[block, 0, field, z]
                elif quarter == 3:
                    middle = own_in[block, 1, field, z - HALO - depth]
                else:
                    middle = own[block, field, z - HALO]
                middle = swap(middle)
                if quarter in (0, 3):
                    away = HALO - z if quarter == 0 else z - HALO - depth + 1
                    low = corners_in[block, 0, quarter // 3, field]
                    high = corners_in[block, 1, quarter // 3, field]
                    if away == 2:
                        low, high = swap(low), swap(high)
                    if away == 3:
                        low, high = pltpu.roll(low, 6, 0), pltpu.roll(high, 2, 0)
                else:
                    low = edges_in[block, 0, quarter - 1, field, i]
                    high = edges_in[block, 1, quarter - 1, field, i]
                    low = swap(low) if late else low
                    high = high if late else swap(high)
                target[field, z, 0:8] = jnp.where(upper, low, middle)
                target[field, z, 8:16] = jnp.where(upper, middle, high)
            return carry

        lax.fori_loop(0, 4, of_field, 0)

    def sweep(source, target, first_plane, last_plane):
        def two_planes(pair, carry):
            for extra in range(2):
                z = first_plane + 2 * pair + extra
                sums = []
                for field in range(4):
                    value = source[field, z]
                    around = pltpu.roll(value, 1, 0) + pltpu.roll(value, 15, 0)
                    around += pltpu.roll(value, 1, 1) + pltpu.roll(value, width - 1, 1)
                    sums.append(around + (source[field, z - 1] + source[field, z + 1]))
                real, imag = box_coupling[2, z], box_coupling[3, z]
                target[0, z] = base[0, z] + box_coupling[0, z] * sums[0]
                target[1, z] = base[1, z] + box_coupling[1, z] * sums[1]
                target[2, z] = base[2, z] + real * sums[2] + imag * sums[3]
                target[3, z] = base[3, z] + real * sums[3] - imag * sums[2]
            return carry

        lax.fori_loop(0, (last_plane - first_plane) // 2, two_planes, 0)

    halos = []
    for block in range(BLOCKS):
        put_edges(block)
        copies = block_copies(block)
        halos += copies
        for copy in copies:
            copy.start()
        for copy in copies:
            copy.wait_recv()
        source = base if block == 0 else sol.at[0]
        assemble(block, source)
        for step in range(HALO):
            target = sol.at[(step + 1) % 2]
            sweep(source, target, step + 1, depth + 2 * HALO - 1 - step)
            source = target

        def take_own(field, carry):
            for z in range(depth):
                own[block + 1, field, z] = jnp.where(
                    upper,
                    swap(sol[0, field, HALO + z, 0:8]),
                    swap(sol[0, field, HALO + z, 8:16]),
                )
            return carry

        lax.fori_loop(0, 4, take_own, 0)

    for z in range(depth):
        zero, two, real, imag = (own[BLOCKS, field, z] for field in range(4))
        plus, minus = zero + two, zero - two
        back = (plus + 2.0 * real, minus - 2.0 * imag, plus - 2.0 * real, minus + 2.0 * imag)
        for n in range(4):
            result[n, z] = chunk[n, z] - back[n] * (0.25 * alpha_wrap ** (-n / 4))
    returns = []
    for ahead in (2, 1, 3):
        other = lax.rem(t + ahead, 4)
        returns.append(
            pltpu.make_async_remote_copy(
                src_ref=result.at[other],
                dst_ref=out_ref.at[:, my_rows, :],
                send_sem=back_send.at[ahead],
                recv_sem=back_recv.at[4 - ahead],
                device_id=(other, s),
                device_id_type=MESH,
            )
        )
    for copy in returns:
        copy.start()
    keep = pltpu.make_async_copy(result.at[t], out_ref.at[:, my_rows, :], local_sem.at[5])
    keep.start()
    for copy in sends + class_sends + halos:
        copy.wait_send()
    keep.wait()
    for copy in returns:
        copy.wait()


def fused_shards(state, initial, labels, mobility_table):
    _, depth, rows, width = state.shape
    slabs = lax.axis_size("space")
    f32 = jnp.float32
    dma = pltpu.SemaphoreType.DMA
    new_state = pl.pallas_call(
        functools.partial(paradiag_kernel, slabs),
        out_shape=jax.ShapeDtypeStruct((depth, rows, width), f32),
        in_specs=[pl.BlockSpec(memory_space=pltpu.SMEM)] + [pl.BlockSpec(memory_space=pltpu.HBM)] * 3,
        out_specs=pl.BlockSpec(memory_space=pltpu.VMEM),
        scratch_shapes=[
            pltpu.VMEM((depth, rows, width), f32),
            pltpu.VMEM((4, depth, 8, width), f32),
            pltpu.VMEM((depth, 8, width), f32),
            pltpu.VMEM((depth + 2 * HALO, 3, 8, width), jnp.int32),
            pltpu.VMEM((4, 2, depth, width), f32),
            pltpu.VMEM((4, 2, depth, width), f32),
            pltpu.VMEM((4, 2, 8, width), f32),
            pltpu.VMEM((5, depth, 8, width), f32),
            pltpu.VMEM((4, depth + 2 * HALO, 16, width), f32),
            pltpu.VMEM((4, depth + 2 * HALO, 16, width), f32),
            pltpu.VMEM((2, 4, depth + 2 * HALO, 16, width), f32),
            pltpu.VMEM((BLOCKS + 1, 4, depth, 8, width), f32),
            pltpu.VMEM((BLOCKS, 2, 4, HALO, 8, width), f32),
            pltpu.VMEM((BLOCKS, 2, 2, 4, 2, 8, width), f32),
            pltpu.VMEM((BLOCKS, 2, 2, 4, 2, 8, width), f32),
            pltpu.VMEM((BLOCKS, 2, 2, 4, 8, width), f32),
            pltpu.VMEM((BLOCKS, 2, 2, 4, 8, width), f32),
            pltpu.VMEM((4, depth, 8, width), f32),
            dma((9,)),
            dma((4,)),
            dma((4,)),
            dma((4,)),
            dma((4,)),
            dma((4, 2)),
            dma((4, 2)),
            dma((3, 2)),
            dma((3, 2)),
            dma((BLOCKS, 8)),
            dma((BLOCKS, 8)),
            dma((4,)),
            dma((4,)),
        ],
        compiler_params=pltpu.CompilerParams(
            collective_id=0, has_side_effects=True, vmem_limit_bytes=40 * 2**20
        ),
    )(mobility_table, state, initial, labels)
    return new_state[None]


def solution(mesh):
    in_specs = (P("tm", "space", None, None), P("space", None, None), P("space", None, None), P())
    out_specs = P("tm", "space", None, None)
    body = fused_shards if mesh.shape["tm"] == 4 and mesh.shape["space"] > 2 else shards
    return jax.shard_map(body, mesh=mesh, in_specs=in_specs, out_specs=out_specs, check_vma=False)
```

```python
import functools
import math

import jax
import jax.numpy as jnp
from jax import lax
from jax.experimental import pallas as pl
from jax.experimental.pallas import tpu as pltpu
from jax.sharding import PartitionSpec as P

MESH = pl.DeviceIdType.MESH
SWEEPS = 8
HALO = 4
BLOCKS = SWEEPS // HALO
GRAINS = 16


alpha_wrap = 0.1
tau_step = 0.25
kappa_grad = 4.0
diag_extra = 6.5


def passed_along(array, axis, by):
    devices = lax.axis_size(axis)
    pairs = [(i, i + by) for i in range(devices) if 0 <= i + by < devices]
    return lax.ppermute(array, axis, pairs)


def extended(cells, sides, width):
    for axis, dim in sides:
        count = lax.axis_size(axis)
        head = lax.slice_in_dim(cells, 0, width, axis=dim)
        tail = lax.slice_in_dim(cells, cells.shape[dim] - width, cells.shape[dim], axis=dim)
        cells = jnp.concatenate(
            [
                lax.ppermute(tail, axis, [(i, (i + 1) % count) for i in range(count)]),
                cells,
                lax.ppermute(head, axis, [((i + 1) % count, i) for i in range(count)]),
            ],
            axis=dim,
        )
    return cells


def partner_2(value, axis, apart):
    mask = 2**apart
    pairs = [(source, source ^ mask) for source in range(lax.axis_size(axis))]
    return lax.ppermute(value, axis, pairs)


def plane_sum(grid_field):
    summed = jnp.roll(grid_field, 1, -2) + jnp.roll(grid_field, -1, -2)
    return summed + jnp.roll(grid_field, 1, -1) + jnp.roll(grid_field, -1, -1)


def mobility_of(labels, rate_table):

    def add_grain(grain_id, summed):
        return summed + jnp.where(
            labels == grain_id, rate_table[grain_id], jnp.zeros((), rate_table.dtype)
        )

    return lax.fori_loop(0, GRAINS, add_grain, jnp.zeros(labels.shape, rate_table.dtype))


def complex_times(left_val, right_val):
    return jnp.stack(
        [
            left_val[0] * right_val[0] - left_val[1] * right_val[1],
            left_val[0] * right_val[1] + left_val[1] * right_val[0],
        ]
    )


def sweep_once(padded, spectral_rhs, inverse_diag, mobility):
    middle = padded[:, 1:-1]
    summed = spectral_rhs + mobility * (padded[:, 2:] + padded[:, :-2] + plane_sum(middle))
    return complex_times(summed, inverse_diag)


def inverse_of(mobility, freq_angle, beta_root):
    diag_real = 1.0 - beta_root * jnp.cos(freq_angle) + diag_extra * mobility
    diag_imag = beta_root * jnp.sin(freq_angle)
    magnitude = diag_real * diag_real + diag_imag * diag_imag
    return jnp.stack([diag_real / magnitude, -diag_imag / magnitude])


def shards(state, initial, labels, mobility_table):
    time_count = lax.axis_size("tm")
    section_count = time_count.bit_length() - 1
    time_index = lax.axis_index("tm")
    index_float = time_index.astype(jnp.float32)
    angle_unit = 2.0 * math.pi / time_count
    gamma_here = alpha_wrap ** (index_float / time_count)
    current = state[0]
    mobility = mobility_of(labels, mobility_table)
    earlier = passed_along(state, "tm", 1)
    earlier_step = jnp.where(time_index == 0, initial, earlier[0])
    padded = extended(current, (("space", 0),), 1)
    laplacian = padded[2:] + padded[:-2] + plane_sum(current) - 6.0 * current
    residual = (
        current
        - earlier_step
        + tau_step * mobility * (current * current * current - current - kappa_grad * laplacian)
    )
    top_bit = section_count - 1
    half_span = 2**top_bit
    local_part = residual * gamma_here
    partner = partner_2(local_part, "tm", top_bit)
    upper_half = time_index // half_span % 2 == 1
    twist_angle = -math.pi * (time_index % half_span).astype(jnp.float32) / half_span
    difference = partner - local_part
    spectral_rhs = jnp.stack(
        [
            jnp.where(upper_half, difference * jnp.cos(twist_angle), local_part + partner),
            jnp.where(upper_half, difference * jnp.sin(twist_angle), jnp.zeros_like(local_part)),
        ]
    )
    for bit_number in range(top_bit - 1, -1, -1):
        half_span = 2**bit_number
        partner = partner_2(spectral_rhs, "tm", bit_number)
        upper_half = time_index // half_span % 2 == 1
        twist_angle = -math.pi * (time_index % half_span).astype(jnp.float32) / half_span
        twiddle = jnp.stack([jnp.cos(twist_angle), jnp.sin(twist_angle)])
        spectral_rhs = jnp.where(
            upper_half, complex_times(partner - spectral_rhs, twiddle), spectral_rhs + partner
        )
    frequency = jnp.zeros((), jnp.int32)
    for bit_number in range(section_count):
        frequency = frequency + time_index // 2**bit_number % 2 * 2 ** (
            section_count - 1 - bit_number
        )
    beta_root = alpha_wrap ** (1.0 / time_count)
    freq_angle = frequency.astype(jnp.float32) * angle_unit
    inverse_diag = inverse_of(mobility, freq_angle, beta_root)
    spectral_sol = complex_times(spectral_rhs, inverse_diag)
    for sweep_index in range(SWEEPS):
        padded_sol = extended(spectral_sol, (("space", 1),), 1)
        spectral_sol = sweep_once(padded_sol, spectral_rhs, inverse_diag, mobility)
    for bit_number in range(section_count):
        half_span = 2**bit_number
        partner = partner_2(spectral_sol, "tm", bit_number)
        upper_half = time_index // half_span % 2 == 1
        twist_angle = math.pi * (time_index % half_span).astype(jnp.float32) / half_span
        twiddle = jnp.stack([jnp.cos(twist_angle), jnp.sin(twist_angle)])
        spectral_sol = jnp.where(
            upper_half,
            partner - complex_times(spectral_sol, twiddle),
            spectral_sol + complex_times(partner, twiddle),
        )
    correction = (spectral_sol[0] / (time_count * gamma_here))[None]
    return state - correction


def ring_place(index):
    return index + index // 2 * (5 - 2 * index)


def grain_rates(labels, table_ref):
    rate = jnp.zeros(labels.shape, jnp.float32)
    for grain_id in range(GRAINS):
        rate = jnp.where(labels == grain_id, table_ref[grain_id], rate)
    return rate


def paradiag_kernel(
    slabs,
    table_ref,
    state_ref,
    initial_ref,
    labels_ref,
    out_ref,
    home,
    chunk,
    first,
    classes,
    rows_out,
    rows_in,
    planes_in,
    coupling,
    box_coupling,
    base,
    sol,
    own,
    own_in,
    edges,
    edges_in,
    corners,
    corners_in,
    result,
    local_sem,
    a2a_send,
    a2a_recv,
    rows_send,
    rows_recv,
    planes_send,
    planes_recv,
    class_send,
    class_recv,
    halo_send,
    halo_recv,
    back_send,
    back_recv,
):
    t = lax.axis_index("tm")
    s = lax.axis_index("space")
    p = ring_place(t)
    below, above = lax.rem(s + slabs - 1, slabs), lax.rem(s + 1, slabs)
    depth, width = home.shape[0], home.shape[2]
    my_rows = pl.ds(pl.multiple_of(p * 8, 8), 8)

    barrier = pltpu.get_barrier_semaphore()
    for ahead in range(1, 4):
        pl.semaphore_signal(
            barrier, inc=1, device_id=(lax.rem(t + ahead, 4), s), device_id_type=MESH
        )
    for ahead in range(4):
        for slab in (below, above):
            pl.semaphore_signal(
                barrier, inc=1, device_id=(lax.rem(t + ahead, 4), slab), device_id_type=MESH
            )

    load_home = pltpu.make_async_copy(state_ref.at[0], home, local_sem.at[0])
    load_home.start()
    chunk_rows = [
        pl.ds(pl.multiple_of(lax.rem(p + shift, 4) * 8, 8), 8) for shift in (3, 0, 1)
    ]
    load_classes = [
        pltpu.make_async_copy(
            labels_ref.at[:, chunk_rows[side], :],
            classes.at[pl.ds(HALO, depth), side],
            local_sem.at[6 + side],
        )
        for side in range(3)
    ]
    for copy in load_classes:
        copy.start()
    load_chunk = pltpu.make_async_copy(
        state_ref.at[0, :, my_rows, :], chunk.at[t], local_sem.at[2]
    )
    load_chunk.start()
    load_first = pltpu.make_async_copy(initial_ref.at[:, my_rows, :], first, local_sem.at[3])
    load_first.start()

    load_home.wait()
    for place in range(4):
        for side, row in enumerate(((8 * place + 31) % 32, (8 * place + 8) % 32)):
            for z in range(depth):
                rows_out[place, side, z : z + 1, :] = home[z, row : row + 1, :]
    load_rows = pltpu.make_async_copy(rows_out.at[p], rows_in.at[t], local_sem.at[4])
    load_rows.start()

    pl.semaphore_wait(barrier, 11)

    sends = []
    for ahead in (2, 1, 3):
        other = lax.rem(t + ahead, 4)
        place = ring_place(other)
        other_rows = pl.ds(pl.multiple_of(place * 8, 8), 8)
        sends.append(
            pltpu.make_async_remote_copy(
                src_ref=home.at[:, other_rows, :],
                dst_ref=chunk.at[t],
                send_sem=a2a_send.at[ahead],
                recv_sem=a2a_recv.at[4 - ahead],
                device_id=(other, s),
                device_id_type=MESH,
            )
        )
        sends.append(
            pltpu.make_async_remote_copy(
                src_ref=rows_out.at[place],
                dst_ref=rows_in.at[t],
                send_sem=rows_send.at[ahead],
                recv_sem=rows_recv.at[4 - ahead],
                device_id=(other, s),
                device_id_type=MESH,
            )
        )
    for ahead in range(4):
        other = lax.rem(t + ahead, 4)
        place = ring_place(other)
        other_rows = pl.ds(pl.multiple_of(place * 8, 8), 8)
        for side, (slab, plane) in enumerate(((above, depth - 1), (below, 0))):
            sends.append(
                pltpu.make_async_remote_copy(
                    src_ref=home.at[plane, other_rows, :],
                    dst_ref=planes_in.at[t, side],
                    send_sem=planes_send.at[ahead, side],
                    recv_sem=planes_recv.at[(4 - ahead) % 4, side],
                    device_id=(other, slab),
                    device_id_type=MESH,
                )
            )
    class_sends = []
    for side in range(3):
        for way, (slab, start, place) in enumerate(
            ((above, depth - HALO, 0), (below, 0, HALO + depth))
        ):
            class_sends.append(
                pltpu.make_async_remote_copy(
                    src_ref=labels_ref.at[pl.ds(start, HALO), chunk_rows[side], :],
                    dst_ref=classes.at[pl.ds(place, HALO), side],
                    send_sem=class_send.at[side, way],
                    recv_sem=class_recv.at[side, way],
                    device_id=(t, slab),
                    device_id_type=MESH,
                )
            )
    for copy in sends + class_sends:
        copy.start()

    row_number = lax.broadcasted_iota(jnp.int32, (8, width), 0)
    top, bottom = row_number == 0, row_number == 7
    upper = row_number < 4
    beta = alpha_wrap**0.25

    for copy in load_classes:
        copy.wait()
    for z in range(depth):
        rate = grain_rates(classes[HALO + z, 1], table_ref)
        real_part = 1.0 + diag_extra * rate
        scale = 1.0 / (real_part * real_part + beta * beta)
        coupling[0, z] = 1.0 / (real_part - beta)
        coupling[1, z] = 1.0 / (real_part + beta)
        coupling[2, z] = real_part * scale
        coupling[3, z] = -beta * scale
        coupling[4, z] = rate

    for copy in class_sends:
        copy.wait_recv()

    def swap(value):
        return pltpu.roll(value, 4, 0)

    def box_plane(z, carry):
        middle = swap(classes[z, 1])
        for part, label in enumerate(
            (
                jnp.where(upper, swap(classes[z, 0]), middle),
                jnp.where(upper, middle, swap(classes[z, 2])),
            )
        ):
            rate = grain_rates(label, table_ref)
            real_part = 1.0 + diag_extra * rate
            scale = rate / (real_part * real_part + beta * beta)
            rows = slice(8 * part, 8 * part + 8)
            box_coupling[0, z, rows] = rate / (real_part - beta)
            box_coupling[1, z, rows] = rate / (real_part + beta)
            box_coupling[2, z, rows] = real_part * scale
            box_coupling[3, z, rows] = beta * scale
        return carry

    lax.fori_loop(0, depth + 2 * HALO, box_plane, 0)

    load_first.wait()
    load_chunk.wait()
    load_rows.wait()
    for copy in sends:
        copy.wait_recv()

    def plane_neighbours(value, row_before, row_after):
        summed = jnp.where(top, row_before, pltpu.roll(value, 1, 0))
        summed += jnp.where(bottom, row_after, pltpu.roll(value, 7, 0))
        return summed + (pltpu.roll(value, 1, 1) + pltpu.roll(value, width - 1, 1))

    for z in range(depth):
        rate = coupling[4, z]
        scaled = []
        for n in range(4):
            value = chunk[n, z]
            around = plane_neighbours(
                value, rows_in[n, 0, z : z + 1, :], rows_in[n, 1, z : z + 1, :]
            )
            around += chunk[n, z - 1] if z > 0 else planes_in[n, 0]
            around += chunk[n, z + 1] if z < depth - 1 else planes_in[n, 1]
            earlier = chunk[n - 1, z] if n > 0 else first[z]
            laplacian = around - 6.0 * value
            residual = (
                value
                - earlier
                + tau_step * rate * (value * value * value - value - kappa_grad * laplacian)
            )
            scaled.append(residual * alpha_wrap ** (n / 4))
        even, odd = scaled[0] + scaled[2], scaled[1] + scaled[3]
        rhs_real, rhs_imag = scaled[0] - scaled[2], scaled[3] - scaled[1]
        inv_real, inv_imag = coupling[2, z], coupling[3, z]
        starts = (
            (even + odd) * coupling[0, z],
            (even - odd) * coupling[1, z],
            rhs_real * inv_real - rhs_imag * inv_imag,
            rhs_real * inv_imag + rhs_imag * inv_real,
        )
        for field in range(4):
            own[0, field, z] = starts[field]

    before, after = ring_place(lax.rem(p + 3, 4)), ring_place(lax.rem(p + 1, 4))

    def block_copies(block):
        moves = []
        for side, (slab, start) in enumerate(((above, depth - HALO), (below, 0))):
            moves.append(
                (own.at[block, :, pl.ds(start, HALO)], own_in.at[block, side], (t, slab))
            )
        for side, other in enumerate((after, before)):
            moves.append(
                (edges.at[block, side], edges_in.at[block, side], (other, s))
            )
            for slab, half, place in ((above, 1, 0), (below, 0, 1)):
                moves.append(
                    (
                        corners.at[block, side, half],
                        corners_in.at[block, side, place],
                        (other, slab),
                    )
                )
        return [
            pltpu.make_async_remote_copy(
                src_ref=source,
                dst_ref=target,
                send_sem=halo_send.at[block, number],
                recv_sem=halo_recv.at[block, number],
                device_id=device,
                device_id_type=MESH,
            )
            for number, (source, target, device) in enumerate(moves)
        ]

    def put_edges(block):
        def of_field(field, carry):
            for half in range(2):
                for i in range(2):
                    one = own[block, field, 4 * half + i]
                    two = own[block, field, 4 * half + i + 2]
                    edges[block, 0, half, field, i] = jnp.where(upper, swap(one), two)
                    edges[block, 1, half, field, i] = jnp.where(upper, one, swap(two))
            for half, nearest in enumerate(((0, 1, 2), (depth - 1, depth - 2, depth - 3))):
                one, two, three = (own[block, field, z] for z in nearest)
                two_three = jnp.where(row_number == 5, pltpu.roll(three, 6, 0), two)
                corners[block, 0, half, field] = jnp.where(upper, swap(one), two_three)
                two_three = jnp.where(row_number == 2, pltpu.roll(three, 2, 0), two)
                corners[block, 1, half, field] = jnp.where(upper, two_three, swap(one))
            return carry

        lax.fori_loop(0, 4, of_field, 0)

    def assemble(block, target):
        def of_field(field, carry):
            for z in range(depth + 2 * HALO):
                quarter, late, i = z // 4, z % 4 // 2, z % 2
                if quarter == 0:
                    middle = own_in[block, 0, field, z]
                elif quarter == 3:
                    middle = own_in[block, 1, field, z - HALO - depth]
                else:
                    middle = own[block, field, z - HALO]
                middle = swap(middle)
                if quarter in (0, 3):
                    away = HALO - z if quarter == 0 else z - HALO - depth + 1
                    low = corners_in[block, 0, quarter // 3, field]
                    high = corners_in[block, 1, quarter // 3, field]
                    if away == 2:
                        low, high = swap(low), swap(high)
                    if away == 3:
                        low, high = pltpu.roll(low, 6, 0), pltpu.roll(high, 2, 0)
                else:
                    low = edges_in[block, 0, quarter - 1, field, i]
                    high = edges_in[block, 1, quarter - 1, field, i]
                    low = swap(low) if late else low
                    high = high if late else swap(high)
                target[field, z, 0:8] = jnp.where(upper, low, middle)
                target[field, z, 8:16] = jnp.where(upper, middle, high)
            return carry

        lax.fori_loop(0, 4, of_field, 0)

    def sweep(source, target, first_plane, last_plane):
        def two_planes(pair, carry):
            for extra in range(2):
                z = first_plane + 2 * pair + extra
                sums = []
                for field in range(4):
                    value = source[field, z]
                    around = pltpu.roll(value, 1, 0) + pltpu.roll(value, 15, 0)
                    around += pltpu.roll(value, 1, 1) + pltpu.roll(value, width - 1, 1)
                    sums.append(around + (source[field, z - 1] + source[field, z + 1]))
                real, imag = box_coupling[2, z], box_coupling[3, z]
                target[0, z] = base[0, z] + box_coupling[0, z] * sums[0]
                target[1, z] = base[1, z] + box_coupling[1, z] * sums[1]
                target[2, z] = base[2, z] + real * sums[2] + imag * sums[3]
                target[3, z] = base[3, z] + real * sums[3] - imag * sums[2]
            return carry

        lax.fori_loop(0, (last_plane - first_plane) // 2, two_planes, 0)

    halos = []
    for block in range(BLOCKS):
        put_edges(block)
        copies = block_copies(block)
        halos += copies
        for copy in copies:
            copy.start()
        for copy in copies:
            copy.wait_recv()
        source = base if block == 0 else sol.at[0]
        assemble(block, source)
        for step in range(HALO):
            target = sol.at[(step + 1) % 2]
            sweep(source, target, step + 1, depth + 2 * HALO - 1 - step)
            source = target

        def take_own(field, carry):
            for z in range(depth):
                own[block + 1, field, z] = jnp.where(
                    upper,
                    swap(sol[0, field, HALO + z, 0:8]),
                    swap(sol[0, field, HALO + z, 8:16]),
                )
            return carry

        lax.fori_loop(0, 4, take_own, 0)

    for z in range(depth):
        zero, two, real, imag = (own[BLOCKS, field, z] for field in range(4))
        plus, minus = zero + two, zero - two
        back = (plus + 2.0 * real, minus - 2.0 * imag, plus - 2.0 * real, minus + 2.0 * imag)
        for n in range(4):
            result[n, z] = chunk[n, z] - back[n] * (0.25 * alpha_wrap ** (-n / 4))
    returns = []
    for ahead in (2, 1, 3):
        other = lax.rem(t + ahead, 4)
        returns.append(
            pltpu.make_async_remote_copy(
                src_ref=result.at[other],
                dst_ref=out_ref.at[:, my_rows, :],
                send_sem=back_send.at[ahead],
                recv_sem=back_recv.at[4 - ahead],
                device_id=(other, s),
                device_id_type=MESH,
            )
        )
    for copy in returns:
        copy.start()
    keep = pltpu.make_async_copy(result.at[t], out_ref.at[:, my_rows, :], local_sem.at[5])
    keep.start()
    for copy in sends + class_sends + halos:
        copy.wait_send()
    keep.wait()
    for copy in returns:
        copy.wait()


def fused_shards(state, initial, labels, mobility_table):
    _, depth, rows, width = state.shape
    slabs = lax.axis_size("space")
    f32 = jnp.float32
    dma = pltpu.SemaphoreType.DMA
    new_state = pl.pallas_call(
        functools.partial(paradiag_kernel, slabs),
        out_shape=jax.ShapeDtypeStruct((depth, rows, width), f32),
        in_specs=[pl.BlockSpec(memory_space=pltpu.SMEM)] + [pl.BlockSpec(memory_space=pltpu.HBM)] * 3,
        out_specs=pl.BlockSpec(memory_space=pltpu.VMEM),
        scratch_shapes=[
            pltpu.VMEM((depth, rows, width), f32),
            pltpu.VMEM((4, depth, 8, width), f32),
            pltpu.VMEM((depth, 8, width), f32),
            pltpu.VMEM((depth + 2 * HALO, 3, 8, width), jnp.int32),
            pltpu.VMEM((4, 2, depth, width), f32),
            pltpu.VMEM((4, 2, depth, width), f32),
            pltpu.VMEM((4, 2, 8, width), f32),
            pltpu.VMEM((5, depth, 8, width), f32),
            pltpu.VMEM((4, depth + 2 * HALO, 16, width), f32),
            pltpu.VMEM((4, depth + 2 * HALO, 16, width), f32),
            pltpu.VMEM((2, 4, depth + 2 * HALO, 16, width), f32),
            pltpu.VMEM((BLOCKS + 1, 4, depth, 8, width), f32),
            pltpu.VMEM((BLOCKS, 2, 4, HALO, 8, width), f32),
            pltpu.VMEM((BLOCKS, 2, 2, 4, 2, 8, width), f32),
            pltpu.VMEM((BLOCKS, 2, 2, 4, 2, 8, width), f32),
            pltpu.VMEM((BLOCKS, 2, 2, 4, 8, width), f32),
            pltpu.VMEM((BLOCKS, 2, 2, 4, 8, width), f32),
            pltpu.VMEM((4, depth, 8, width), f32),
            dma((9,)),
            dma((4,)),
            dma((4,)),
            dma((4,)),
            dma((4,)),
            dma((4, 2)),
            dma((4, 2)),
            dma((3, 2)),
            dma((3, 2)),
            dma((BLOCKS, 8)),
            dma((BLOCKS, 8)),
            dma((4,)),
            dma((4,)),
        ],
        compiler_params=pltpu.CompilerParams(
            collective_id=0, has_side_effects=True, vmem_limit_bytes=60 * 2**20
        ),
    )(mobility_table, state, initial, labels)
    return new_state[None]


def solution(mesh):
    in_specs = (P("tm", "space", None, None), P("space", None, None), P("space", None, None), P())
    out_specs = P("tm", "space", None, None)
    body = fused_shards if mesh.shape["tm"] == 4 and mesh.shape["space"] > 2 else shards
    return jax.shard_map(body, mesh=mesh, in_specs=in_specs, out_specs=out_specs, check_vma=False)
```

```python
import functools
import math

import jax
import jax.numpy as jnp
from jax import lax
from jax.experimental import pallas as pl
from jax.experimental.pallas import tpu as pltpu
from jax.sharding import PartitionSpec as P

MESH = pl.DeviceIdType.MESH
SWEEPS = 8
HALO = 4
BLOCKS = SWEEPS // HALO
GRAINS = 16


alpha_wrap = 0.1
tau_step = 0.25
kappa_grad = 4.0
diag_extra = 6.5


def passed_along(array, axis, by):
    devices = lax.axis_size(axis)
    pairs = [(i, i + by) for i in range(devices) if 0 <= i + by < devices]
    return lax.ppermute(array, axis, pairs)


def extended(cells, sides, width):
    for axis, dim in sides:
        count = lax.axis_size(axis)
        head = lax.slice_in_dim(cells, 0, width, axis=dim)
        tail = lax.slice_in_dim(cells, cells.shape[dim] - width, cells.shape[dim], axis=dim)
        cells = jnp.concatenate(
            [
                lax.ppermute(tail, axis, [(i, (i + 1) % count) for i in range(count)]),
                cells,
                lax.ppermute(head, axis, [((i + 1) % count, i) for i in range(count)]),
            ],
            axis=dim,
        )
    return cells


def partner_2(value, axis, apart):
    mask = 2**apart
    pairs = [(source, source ^ mask) for source in range(lax.axis_size(axis))]
    return lax.ppermute(value, axis, pairs)


def plane_sum(grid_field):
    summed = jnp.roll(grid_field, 1, -2) + jnp.roll(grid_field, -1, -2)
    return summed + jnp.roll(grid_field, 1, -1) + jnp.roll(grid_field, -1, -1)


def mobility_of(labels, rate_table):

    def add_grain(grain_id, summed):
        return summed + jnp.where(
            labels == grain_id, rate_table[grain_id], jnp.zeros((), rate_table.dtype)
        )

    return lax.fori_loop(0, GRAINS, add_grain, jnp.zeros(labels.shape, rate_table.dtype))


def complex_times(left_val, right_val):
    return jnp.stack(
        [
            left_val[0] * right_val[0] - left_val[1] * right_val[1],
            left_val[0] * right_val[1] + left_val[1] * right_val[0],
        ]
    )


def sweep_once(padded, spectral_rhs, inverse_diag, mobility):
    middle = padded[:, 1:-1]
    summed = spectral_rhs + mobility * (padded[:, 2:] + padded[:, :-2] + plane_sum(middle))
    return complex_times(summed, inverse_diag)


def inverse_of(mobility, freq_angle, beta_root):
    diag_real = 1.0 - beta_root * jnp.cos(freq_angle) + diag_extra * mobility
    diag_imag = beta_root * jnp.sin(freq_angle)
    magnitude = diag_real * diag_real + diag_imag * diag_imag
    return jnp.stack([diag_real / magnitude, -diag_imag / magnitude])


def shards(state, initial, labels, mobility_table):
    time_count = lax.axis_size("tm")
    section_count = time_count.bit_length() - 1
    time_index = lax.axis_index("tm")
    index_float = time_index.astype(jnp.float32)
    angle_unit = 2.0 * math.pi / time_count
    gamma_here = alpha_wrap ** (index_float / time_count)
    current = state[0]
    mobility = mobility_of(labels, mobility_table)
    earlier = passed_along(state, "tm", 1)
    earlier_step = jnp.where(time_index == 0, initial, earlier[0])
    padded = extended(current, (("space", 0),), 1)
    laplacian = padded[2:] + padded[:-2] + plane_sum(current) - 6.0 * current
    residual = (
        current
        - earlier_step
        + tau_step * mobility * (current * current * current - current - kappa_grad * laplacian)
    )
    top_bit = section_count - 1
    half_span = 2**top_bit
    local_part = residual * gamma_here
    partner = partner_2(local_part, "tm", top_bit)
    upper_half = time_index // half_span % 2 == 1
    twist_angle = -math.pi * (time_index % half_span).astype(jnp.float32) / half_span
    difference = partner - local_part
    spectral_rhs = jnp.stack(
        [
            jnp.where(upper_half, difference * jnp.cos(twist_angle), local_part + partner),
            jnp.where(upper_half, difference * jnp.sin(twist_angle), jnp.zeros_like(local_part)),
        ]
    )
    for bit_number in range(top_bit - 1, -1, -1):
        half_span = 2**bit_number
        partner = partner_2(spectral_rhs, "tm", bit_number)
        upper_half = time_index // half_span % 2 == 1
        twist_angle = -math.pi * (time_index % half_span).astype(jnp.float32) / half_span
        twiddle = jnp.stack([jnp.cos(twist_angle), jnp.sin(twist_angle)])
        spectral_rhs = jnp.where(
            upper_half, complex_times(partner - spectral_rhs, twiddle), spectral_rhs + partner
        )
    frequency = jnp.zeros((), jnp.int32)
    for bit_number in range(section_count):
        frequency = frequency + time_index // 2**bit_number % 2 * 2 ** (
            section_count - 1 - bit_number
        )
    beta_root = alpha_wrap ** (1.0 / time_count)
    freq_angle = frequency.astype(jnp.float32) * angle_unit
    inverse_diag = inverse_of(mobility, freq_angle, beta_root)
    spectral_sol = complex_times(spectral_rhs, inverse_diag)
    for sweep_index in range(SWEEPS):
        padded_sol = extended(spectral_sol, (("space", 1),), 1)
        spectral_sol = sweep_once(padded_sol, spectral_rhs, inverse_diag, mobility)
    for bit_number in range(section_count):
        half_span = 2**bit_number
        partner = partner_2(spectral_sol, "tm", bit_number)
        upper_half = time_index // half_span % 2 == 1
        twist_angle = math.pi * (time_index % half_span).astype(jnp.float32) / half_span
        twiddle = jnp.stack([jnp.cos(twist_angle), jnp.sin(twist_angle)])
        spectral_sol = jnp.where(
            upper_half,
            partner - complex_times(spectral_sol, twiddle),
            spectral_sol + complex_times(partner, twiddle),
        )
    correction = (spectral_sol[0] / (time_count * gamma_here))[None]
    return state - correction


def ring_place(index):
    return index + index // 2 * (5 - 2 * index)


def grain_rates(labels, table_ref):
    rate = jnp.zeros(labels.shape, jnp.float32)
    for grain_id in range(GRAINS):
        rate = jnp.where(labels == grain_id, table_ref[grain_id], rate)
    return rate


def paradiag_kernel(
    slabs,
    table_ref,
    state_ref,
    initial_ref,
    labels_ref,
    out_ref,
    home,
    chunk,
    first,
    classes,
    rows_out,
    rows_in,
    planes_in,
    coupling,
    box_coupling,
    base,
    sol,
    own,
    own_in,
    edges,
    edges_in,
    corners,
    corners_in,
    result,
    local_sem,
    a2a_send,
    a2a_recv,
    rows_send,
    rows_recv,
    planes_send,
    planes_recv,
    class_send,
    class_recv,
    halo_send,
    halo_recv,
    back_send,
    back_recv,
):
    t = lax.axis_index("tm")
    s = lax.axis_index("space")
    p = ring_place(t)
    below, above = lax.rem(s + slabs - 1, slabs), lax.rem(s + 1, slabs)
    depth, width = home.shape[0], home.shape[2]
    my_rows = pl.ds(pl.multiple_of(p * 8, 8), 8)

    barrier = pltpu.get_barrier_semaphore()
    for ahead in range(1, 4):
        pl.semaphore_signal(
            barrier, inc=1, device_id=(lax.rem(t + ahead, 4), s), device_id_type=MESH
        )
    for ahead in range(4):
        for slab in (below, above):
            pl.semaphore_signal(
                barrier, inc=1, device_id=(lax.rem(t + ahead, 4), slab), device_id_type=MESH
            )

    load_home = pltpu.make_async_copy(state_ref.at[0], home, local_sem.at[0])
    load_home.start()
    chunk_rows = [
        pl.ds(pl.multiple_of(lax.rem(p + shift, 4) * 8, 8), 8) for shift in (3, 0, 1)
    ]
    load_classes = [
        pltpu.make_async_copy(
            labels_ref.at[:, chunk_rows[side], :],
            classes.at[pl.ds(HALO, depth), side],
            local_sem.at[6 + side],
        )
        for side in range(3)
    ]
    for copy in load_classes:
        copy.start()
    load_chunk = pltpu.make_async_copy(
        state_ref.at[0, :, my_rows, :], chunk.at[t], local_sem.at[2]
    )
    load_chunk.start()
    load_first = pltpu.make_async_copy(initial_ref.at[:, my_rows, :], first, local_sem.at[3])
    load_first.start()

    pl.semaphore_wait(barrier, 11)

    sends = []
    for ahead in (2, 1, 3):
        other = lax.rem(t + ahead, 4)
        place = ring_place(other)
        other_rows = pl.ds(pl.multiple_of(place * 8, 8), 8)
        sends.append(
            pltpu.make_async_remote_copy(
                src_ref=state_ref.at[0, :, other_rows, :],
                dst_ref=chunk.at[t],
                send_sem=a2a_send.at[ahead],
                recv_sem=a2a_recv.at[4 - ahead],
                device_id=(other, s),
                device_id_type=MESH,
            )
        )
        sends.append(
            pltpu.make_async_remote_copy(
                src_ref=rows_out.at[place],
                dst_ref=rows_in.at[t],
                send_sem=rows_send.at[ahead],
                recv_sem=rows_recv.at[4 - ahead],
                device_id=(other, s),
                device_id_type=MESH,
            )
        )
    for ahead in range(4):
        other = lax.rem(t + ahead, 4)
        place = ring_place(other)
        other_rows = pl.ds(pl.multiple_of(place * 8, 8), 8)
        for side, (slab, plane) in enumerate(((above, depth - 1), (below, 0))):
            sends.append(
                pltpu.make_async_remote_copy(
                    src_ref=state_ref.at[0, plane, other_rows, :],
                    dst_ref=planes_in.at[t, side],
                    send_sem=planes_send.at[ahead, side],
                    recv_sem=planes_recv.at[(4 - ahead) % 4, side],
                    device_id=(other, slab),
                    device_id_type=MESH,
                )
            )
    class_sends = []
    for side in range(3):
        for way, (slab, start, place) in enumerate(
            ((above, depth - HALO, 0), (below, 0, HALO + depth))
        ):
            class_sends.append(
                pltpu.make_async_remote_copy(
                    src_ref=labels_ref.at[pl.ds(start, HALO), chunk_rows[side], :],
                    dst_ref=classes.at[pl.ds(place, HALO), side],
                    send_sem=class_send.at[side, way],
                    recv_sem=class_recv.at[side, way],
                    device_id=(t, slab),
                    device_id_type=MESH,
                )
            )
    row_sends = sends[1:6:2]
    for copy in sends[0:6:2]:
        copy.start()
    load_home.wait()
    for place in range(4):
        for side, row in enumerate(((8 * place + 31) % 32, (8 * place + 8) % 32)):
            for z in range(depth):
                rows_out[place, side, z : z + 1, :] = home[z, row : row + 1, :]
    load_rows = pltpu.make_async_copy(rows_out.at[p], rows_in.at[t], local_sem.at[4])
    load_rows.start()
    for copy in row_sends + sends[6:] + class_sends:
        copy.start()

    row_number = lax.broadcasted_iota(jnp.int32, (8, width), 0)
    top, bottom = row_number == 0, row_number == 7
    upper = row_number < 4
    beta = alpha_wrap**0.25

    for copy in load_classes:
        copy.wait()
    for z in range(depth):
        rate = grain_rates(classes[HALO + z, 1], table_ref)
        real_part = 1.0 + diag_extra * rate
        scale = 1.0 / (real_part * real_part + beta * beta)
        coupling[0, z] = 1.0 / (real_part - beta)
        coupling[1, z] = 1.0 / (real_part + beta)
        coupling[2, z] = real_part * scale
        coupling[3, z] = -beta * scale
        coupling[4, z] = rate

    for copy in class_sends:
        copy.wait_recv()

    def swap(value):
        return pltpu.roll(value, 4, 0)

    def box_plane(z, carry):
        middle = swap(classes[z, 1])
        for part, label in enumerate(
            (
                jnp.where(upper, swap(classes[z, 0]), middle),
                jnp.where(upper, middle, swap(classes[z, 2])),
            )
        ):
            rate = grain_rates(label, table_ref)
            real_part = 1.0 + diag_extra * rate
            scale = rate / (real_part * real_part + beta * beta)
            rows = slice(8 * part, 8 * part + 8)
            box_coupling[0, z, rows] = rate / (real_part - beta)
            box_coupling[1, z, rows] = rate / (real_part + beta)
            box_coupling[2, z, rows] = real_part * scale
            box_coupling[3, z, rows] = beta * scale
        return carry

    lax.fori_loop(0, depth + 2 * HALO, box_plane, 0)

    load_first.wait()
    load_chunk.wait()
    load_rows.wait()
    for copy in sends:
        copy.wait_recv()

    def plane_neighbours(value, row_before, row_after):
        summed = jnp.where(top, row_before, pltpu.roll(value, 1, 0))
        summed += jnp.where(bottom, row_after, pltpu.roll(value, 7, 0))
        return summed + (pltpu.roll(value, 1, 1) + pltpu.roll(value, width - 1, 1))

    for z in range(depth):
        rate = coupling[4, z]
        scaled = []
        for n in range(4):
            value = chunk[n, z]
            around = plane_neighbours(
                value, rows_in[n, 0, z : z + 1, :], rows_in[n, 1, z : z + 1, :]
            )
            around += chunk[n, z - 1] if z > 0 else planes_in[n, 0]
            around += chunk[n, z + 1] if z < depth - 1 else planes_in[n, 1]
            earlier = chunk[n - 1, z] if n > 0 else first[z]
            laplacian = around - 6.0 * value
            residual = (
                value
                - earlier
                + tau_step * rate * (value * value * value - value - kappa_grad * laplacian)
            )
            scaled.append(residual * alpha_wrap ** (n / 4))
        even, odd = scaled[0] + scaled[2], scaled[1] + scaled[3]
        rhs_real, rhs_imag = scaled[0] - scaled[2], scaled[3] - scaled[1]
        inv_real, inv_imag = coupling[2, z], coupling[3, z]
        starts = (
            (even + odd) * coupling[0, z],
            (even - odd) * coupling[1, z],
            rhs_real * inv_real - rhs_imag * inv_imag,
            rhs_real * inv_imag + rhs_imag * inv_real,
        )
        for field in range(4):
            own[0, field, z] = starts[field]

    before, after = ring_place(lax.rem(p + 3, 4)), ring_place(lax.rem(p + 1, 4))

    def block_copies(block):
        moves = []
        for side, (slab, start) in enumerate(((above, depth - HALO), (below, 0))):
            moves.append(
                (own.at[block, :, pl.ds(start, HALO)], own_in.at[block, side], (t, slab))
            )
        for side, other in enumerate((after, before)):
            moves.append(
                (edges.at[block, side], edges_in.at[block, side], (other, s))
            )
            for slab, half, place in ((above, 1, 0), (below, 0, 1)):
                moves.append(
                    (
                        corners.at[block, side, half],
                        corners_in.at[block, side, place],
                        (other, slab),
                    )
                )
        return [
            pltpu.make_async_remote_copy(
                src_ref=source,
                dst_ref=target,
                send_sem=halo_send.at[block, number],
                recv_sem=halo_recv.at[block, number],
                device_id=device,
                device_id_type=MESH,
            )
            for number, (source, target, device) in enumerate(moves)
        ]

    def put_edges(block):
        def of_field(field, carry):
            for half in range(2):
                for i in range(2):
                    one = own[block, field, 4 * half + i]
                    two = own[block, field, 4 * half + i + 2]
                    edges[block, 0, half, field, i] = jnp.where(upper, swap(one), two)
                    edges[block, 1, half, field, i] = jnp.where(upper, one, swap(two))
            for half, nearest in enumerate(((0, 1, 2), (depth - 1, depth - 2, depth - 3))):
                one, two, three = (own[block, field, z] for z in nearest)
                two_three = jnp.where(row_number == 5, pltpu.roll(three, 6, 0), two)
                corners[block, 0, half, field] = jnp.where(upper, swap(one), two_three)
                two_three = jnp.where(row_number == 2, pltpu.roll(three, 2, 0), two)
                corners[block, 1, half, field] = jnp.where(upper, two_three, swap(one))
            return carry

        lax.fori_loop(0, 4, of_field, 0)

    def assemble(block, target):
        def of_field(field, carry):
            for z in range(depth + 2 * HALO):
                quarter, late, i = z // 4, z % 4 // 2, z % 2
                if quarter == 0:
                    middle = own_in[block, 0, field, z]
                elif quarter == 3:
                    middle = own_in[block, 1, field, z - HALO - depth]
                else:
                    middle = own[block, field, z - HALO]
                middle = swap(middle)
                if quarter in (0, 3):
                    away = HALO - z if quarter == 0 else z - HALO - depth + 1
                    low = corners_in[block, 0, quarter // 3, field]
                    high = corners_in[block, 1, quarter // 3, field]
                    if away == 2:
                        low, high = swap(low), swap(high)
                    if away == 3:
                        low, high = pltpu.roll(low, 6, 0), pltpu.roll(high, 2, 0)
                else:
                    low = edges_in[block, 0, quarter - 1, field, i]
                    high = edges_in[block, 1, quarter - 1, field, i]
                    low = swap(low) if late else low
                    high = high if late else swap(high)
                target[field, z, 0:8] = jnp.where(upper, low, middle)
                target[field, z, 8:16] = jnp.where(upper, middle, high)
            return carry

        lax.fori_loop(0, 4, of_field, 0)

    def sweep(source, target, first_plane, last_plane):
        def two_planes(pair, carry):
            for extra in range(2):
                z = first_plane + 2 * pair + extra
                sums = []
                for field in range(4):
                    value = source[field, z]
                    around = pltpu.roll(value, 1, 0) + pltpu.roll(value, 15, 0)
                    around += pltpu.roll(value, 1, 1) + pltpu.roll(value, width - 1, 1)
                    sums.append(around + (source[field, z - 1] + source[field, z + 1]))
                real, imag = box_coupling[2, z], box_coupling[3, z]
                target[0, z] = base[0, z] + box_coupling[0, z] * sums[0]
                target[1, z] = base[1, z] + box_coupling[1, z] * sums[1]
                target[2, z] = base[2, z] + real * sums[2] + imag * sums[3]
                target[3, z] = base[3, z] + real * sums[3] - imag * sums[2]
            return carry

        lax.fori_loop(0, (last_plane - first_plane) // 2, two_planes, 0)

    halos = []
    for block in range(BLOCKS):
        put_edges(block)
        copies = block_copies(block)
        halos += copies
        for copy in copies:
            copy.start()
        for copy in copies:
            copy.wait_recv()
        source = base if block == 0 else sol.at[0]
        assemble(block, source)
        for step in range(HALO):
            target = sol.at[(step + 1) % 2]
            sweep(source, target, step + 1, depth + 2 * HALO - 1 - step)
            source = target

        def take_own(field, carry):
            for z in range(depth):
                own[block + 1, field, z] = jnp.where(
                    upper,
                    swap(sol[0, field, HALO + z, 0:8]),
                    swap(sol[0, field, HALO + z, 8:16]),
                )
            return carry

        lax.fori_loop(0, 4, take_own, 0)

    for z in range(depth):
        zero, two, real, imag = (own[BLOCKS, field, z] for field in range(4))
        plus, minus = zero + two, zero - two
        back = (plus + 2.0 * real, minus - 2.0 * imag, plus - 2.0 * real, minus + 2.0 * imag)
        for n in range(4):
            result[n, z] = chunk[n, z] - back[n] * (0.25 * alpha_wrap ** (-n / 4))
    returns = []
    for ahead in (2, 1, 3):
        other = lax.rem(t + ahead, 4)
        returns.append(
            pltpu.make_async_remote_copy(
                src_ref=result.at[other],
                dst_ref=out_ref.at[:, my_rows, :],
                send_sem=back_send.at[ahead],
                recv_sem=back_recv.at[4 - ahead],
                device_id=(other, s),
                device_id_type=MESH,
            )
        )
    for copy in returns:
        copy.start()
    keep = pltpu.make_async_copy(result.at[t], out_ref.at[:, my_rows, :], local_sem.at[5])
    keep.start()
    for copy in sends + class_sends + halos:
        copy.wait_send()
    keep.wait()
    for copy in returns:
        copy.wait()


def fused_shards(state, initial, labels, mobility_table):
    _, depth, rows, width = state.shape
    slabs = lax.axis_size("space")
    f32 = jnp.float32
    dma = pltpu.SemaphoreType.DMA
    new_state = pl.pallas_call(
        functools.partial(paradiag_kernel, slabs),
        out_shape=jax.ShapeDtypeStruct((depth, rows, width), f32),
        in_specs=[pl.BlockSpec(memory_space=pltpu.SMEM)] + [pl.BlockSpec(memory_space=pltpu.HBM)] * 3,
        out_specs=pl.BlockSpec(memory_space=pltpu.VMEM),
        scratch_shapes=[
            pltpu.VMEM((depth, rows, width), f32),
            pltpu.VMEM((4, depth, 8, width), f32),
            pltpu.VMEM((depth, 8, width), f32),
            pltpu.VMEM((depth + 2 * HALO, 3, 8, width), jnp.int32),
            pltpu.VMEM((4, 2, depth, width), f32),
            pltpu.VMEM((4, 2, depth, width), f32),
            pltpu.VMEM((4, 2, 8, width), f32),
            pltpu.VMEM((5, depth, 8, width), f32),
            pltpu.VMEM((4, depth + 2 * HALO, 16, width), f32),
            pltpu.VMEM((4, depth + 2 * HALO, 16, width), f32),
            pltpu.VMEM((2, 4, depth + 2 * HALO, 16, width), f32),
            pltpu.VMEM((BLOCKS + 1, 4, depth, 8, width), f32),
            pltpu.VMEM((BLOCKS, 2, 4, HALO, 8, width), f32),
            pltpu.VMEM((BLOCKS, 2, 2, 4, 2, 8, width), f32),
            pltpu.VMEM((BLOCKS, 2, 2, 4, 2, 8, width), f32),
            pltpu.VMEM((BLOCKS, 2, 2, 4, 8, width), f32),
            pltpu.VMEM((BLOCKS, 2, 2, 4, 8, width), f32),
            pltpu.VMEM((4, depth, 8, width), f32),
            dma((9,)),
            dma((4,)),
            dma((4,)),
            dma((4,)),
            dma((4,)),
            dma((4, 2)),
            dma((4, 2)),
            dma((3, 2)),
            dma((3, 2)),
            dma((BLOCKS, 8)),
            dma((BLOCKS, 8)),
            dma((4,)),
            dma((4,)),
        ],
        compiler_params=pltpu.CompilerParams(
            collective_id=0, has_side_effects=True, vmem_limit_bytes=60 * 2**20
        ),
    )(mobility_table, state, initial, labels)
    return new_state[None]


def solution(mesh):
    in_specs = (P("tm", "space", None, None), P("space", None, None), P("space", None, None), P())
    out_specs = P("tm", "space", None, None)
    body = fused_shards if mesh.shape["tm"] == 4 and mesh.shape["space"] > 2 else shards
    return jax.shard_map(body, mesh=mesh, in_specs=in_specs, out_specs=out_specs, check_vma=False)
```

```python
import functools
import math

import jax
import jax.numpy as jnp
from jax import lax
from jax.experimental import pallas as pl
from jax.experimental.pallas import tpu as pltpu
from jax.sharding import PartitionSpec as P

MESH = pl.DeviceIdType.MESH
SWEEPS = 8
HALO = 4
BLOCKS = SWEEPS // HALO
GRAINS = 16


alpha_wrap = 0.1
tau_step = 0.25
kappa_grad = 4.0
diag_extra = 6.5


def passed_along(array, axis, by):
    devices = lax.axis_size(axis)
    pairs = [(i, i + by) for i in range(devices) if 0 <= i + by < devices]
    return lax.ppermute(array, axis, pairs)


def extended(cells, sides, width):
    for axis, dim in sides:
        count = lax.axis_size(axis)
        head = lax.slice_in_dim(cells, 0, width, axis=dim)
        tail = lax.slice_in_dim(cells, cells.shape[dim] - width, cells.shape[dim], axis=dim)
        cells = jnp.concatenate(
            [
                lax.ppermute(tail, axis, [(i, (i + 1) % count) for i in range(count)]),
                cells,
                lax.ppermute(head, axis, [((i + 1) % count, i) for i in range(count)]),
            ],
            axis=dim,
        )
    return cells


def partner_2(value, axis, apart):
    mask = 2**apart
    pairs = [(source, source ^ mask) for source in range(lax.axis_size(axis))]
    return lax.ppermute(value, axis, pairs)


def plane_sum(grid_field):
    summed = jnp.roll(grid_field, 1, -2) + jnp.roll(grid_field, -1, -2)
    return summed + jnp.roll(grid_field, 1, -1) + jnp.roll(grid_field, -1, -1)


def mobility_of(labels, rate_table):

    def add_grain(grain_id, summed):
        return summed + jnp.where(
            labels == grain_id, rate_table[grain_id], jnp.zeros((), rate_table.dtype)
        )

    return lax.fori_loop(0, GRAINS, add_grain, jnp.zeros(labels.shape, rate_table.dtype))


def complex_times(left_val, right_val):
    return jnp.stack(
        [
            left_val[0] * right_val[0] - left_val[1] * right_val[1],
            left_val[0] * right_val[1] + left_val[1] * right_val[0],
        ]
    )


def sweep_once(padded, spectral_rhs, inverse_diag, mobility):
    middle = padded[:, 1:-1]
    summed = spectral_rhs + mobility * (padded[:, 2:] + padded[:, :-2] + plane_sum(middle))
    return complex_times(summed, inverse_diag)


def inverse_of(mobility, freq_angle, beta_root):
    diag_real = 1.0 - beta_root * jnp.cos(freq_angle) + diag_extra * mobility
    diag_imag = beta_root * jnp.sin(freq_angle)
    magnitude = diag_real * diag_real + diag_imag * diag_imag
    return jnp.stack([diag_real / magnitude, -diag_imag / magnitude])


def shards(state, initial, labels, mobility_table):
    time_count = lax.axis_size("tm")
    section_count = time_count.bit_length() - 1
    time_index = lax.axis_index("tm")
    index_float = time_index.astype(jnp.float32)
    angle_unit = 2.0 * math.pi / time_count
    gamma_here = alpha_wrap ** (index_float / time_count)
    current = state[0]
    mobility = mobility_of(labels, mobility_table)
    earlier = passed_along(state, "tm", 1)
    earlier_step = jnp.where(time_index == 0, initial, earlier[0])
    padded = extended(current, (("space", 0),), 1)
    laplacian = padded[2:] + padded[:-2] + plane_sum(current) - 6.0 * current
    residual = (
        current
        - earlier_step
        + tau_step * mobility * (current * current * current - current - kappa_grad * laplacian)
    )
    top_bit = section_count - 1
    half_span = 2**top_bit
    local_part = residual * gamma_here
    partner = partner_2(local_part, "tm", top_bit)
    upper_half = time_index // half_span % 2 == 1
    twist_angle = -math.pi * (time_index % half_span).astype(jnp.float32) / half_span
    difference = partner - local_part
    spectral_rhs = jnp.stack(
        [
            jnp.where(upper_half, difference * jnp.cos(twist_angle), local_part + partner),
            jnp.where(upper_half, difference * jnp.sin(twist_angle), jnp.zeros_like(local_part)),
        ]
    )
    for bit_number in range(top_bit - 1, -1, -1):
        half_span = 2**bit_number
        partner = partner_2(spectral_rhs, "tm", bit_number)
        upper_half = time_index // half_span % 2 == 1
        twist_angle = -math.pi * (time_index % half_span).astype(jnp.float32) / half_span
        twiddle = jnp.stack([jnp.cos(twist_angle), jnp.sin(twist_angle)])
        spectral_rhs = jnp.where(
            upper_half, complex_times(partner - spectral_rhs, twiddle), spectral_rhs + partner
        )
    frequency = jnp.zeros((), jnp.int32)
    for bit_number in range(section_count):
        frequency = frequency + time_index // 2**bit_number % 2 * 2 ** (
            section_count - 1 - bit_number
        )
    beta_root = alpha_wrap ** (1.0 / time_count)
    freq_angle = frequency.astype(jnp.float32) * angle_unit
    inverse_diag = inverse_of(mobility, freq_angle, beta_root)
    spectral_sol = complex_times(spectral_rhs, inverse_diag)
    for sweep_index in range(SWEEPS):
        padded_sol = extended(spectral_sol, (("space", 1),), 1)
        spectral_sol = sweep_once(padded_sol, spectral_rhs, inverse_diag, mobility)
    for bit_number in range(section_count):
        half_span = 2**bit_number
        partner = partner_2(spectral_sol, "tm", bit_number)
        upper_half = time_index // half_span % 2 == 1
        twist_angle = math.pi * (time_index % half_span).astype(jnp.float32) / half_span
        twiddle = jnp.stack([jnp.cos(twist_angle), jnp.sin(twist_angle)])
        spectral_sol = jnp.where(
            upper_half,
            partner - complex_times(spectral_sol, twiddle),
            spectral_sol + complex_times(partner, twiddle),
        )
    correction = (spectral_sol[0] / (time_count * gamma_here))[None]
    return state - correction


def ring_place(index):
    return index + index // 2 * (5 - 2 * index)


def grain_rates(labels, table_ref):
    rate = jnp.zeros(labels.shape, jnp.float32)
    for grain_id in range(GRAINS):
        rate = jnp.where(labels == grain_id, table_ref[grain_id], rate)
    return rate


def paradiag_kernel(
    slabs,
    table_ref,
    state_ref,
    initial_ref,
    labels_ref,
    out_ref,
    home,
    chunk,
    first,
    classes,
    rows_out,
    rows_in,
    planes_in,
    coupling,
    box_coupling,
    base,
    sol,
    own,
    own_in,
    edges,
    edges_in,
    corners,
    corners_in,
    result,
    local_sem,
    a2a_send,
    a2a_recv,
    rows_send,
    rows_recv,
    planes_send,
    planes_recv,
    class_send,
    class_recv,
    halo_send,
    halo_recv,
    back_send,
    back_recv,
):
    t = lax.axis_index("tm")
    s = lax.axis_index("space")
    p = ring_place(t)
    below, above = lax.rem(s + slabs - 1, slabs), lax.rem(s + 1, slabs)
    depth, width = home.shape[0], home.shape[2]
    my_rows = pl.ds(pl.multiple_of(p * 8, 8), 8)

    barrier = pltpu.get_barrier_semaphore()
    for ahead in range(1, 4):
        pl.semaphore_signal(
            barrier, inc=1, device_id=(lax.rem(t + ahead, 4), s), device_id_type=MESH
        )
    for ahead in range(4):
        for slab in (below, above):
            pl.semaphore_signal(
                barrier, inc=1, device_id=(lax.rem(t + ahead, 4), slab), device_id_type=MESH
            )

    load_home = pltpu.make_async_copy(state_ref.at[0], home, local_sem.at[0])
    load_home.start()
    chunk_rows = [
        pl.ds(pl.multiple_of(lax.rem(p + shift, 4) * 8, 8), 8) for shift in (3, 0, 1)
    ]
    load_classes = [
        pltpu.make_async_copy(
            labels_ref.at[:, chunk_rows[side], :],
            classes.at[pl.ds(HALO, depth), side],
            local_sem.at[6 + side],
        )
        for side in range(3)
    ]
    for copy in load_classes:
        copy.start()
    load_chunk = pltpu.make_async_copy(
        state_ref.at[0, :, my_rows, :], chunk.at[t], local_sem.at[2]
    )
    load_chunk.start()
    load_first = pltpu.make_async_copy(initial_ref.at[:, my_rows, :], first, local_sem.at[3])
    load_first.start()

    load_home.wait()
    for place in range(4):
        for side, row in enumerate(((8 * place + 31) % 32, (8 * place + 8) % 32)):
            for z in range(depth):
                rows_out[place, side, z : z + 1, :] = home[z, row : row + 1, :]
    load_rows = pltpu.make_async_copy(rows_out.at[p], rows_in.at[t], local_sem.at[4])
    load_rows.start()

    pl.semaphore_wait(barrier, 11)

    sends = []
    for ahead in (2, 1, 3):
        other = lax.rem(t + ahead, 4)
        place = ring_place(other)
        other_rows = pl.ds(pl.multiple_of(place * 8, 8), 8)
        sends.append(
            pltpu.make_async_remote_copy(
                src_ref=home.at[:, other_rows, :],
                dst_ref=chunk.at[t],
                send_sem=a2a_send.at[ahead],
                recv_sem=a2a_recv.at[4 - ahead],
                device_id=(other, s),
                device_id_type=MESH,
            )
        )
        sends.append(
            pltpu.make_async_remote_copy(
                src_ref=rows_out.at[place],
                dst_ref=rows_in.at[t],
                send_sem=rows_send.at[ahead],
                recv_sem=rows_recv.at[4 - ahead],
                device_id=(other, s),
                device_id_type=MESH,
            )
        )
    for ahead in range(4):
        other = lax.rem(t + ahead, 4)
        place = ring_place(other)
        other_rows = pl.ds(pl.multiple_of(place * 8, 8), 8)
        for side, (slab, plane) in enumerate(((above, depth - 1), (below, 0))):
            sends.append(
                pltpu.make_async_remote_copy(
                    src_ref=home.at[plane, other_rows, :],
                    dst_ref=planes_in.at[t, side],
                    send_sem=planes_send.at[ahead, side],
                    recv_sem=planes_recv.at[(4 - ahead) % 4, side],
                    device_id=(other, slab),
                    device_id_type=MESH,
                )
            )
    class_sends = []
    for side in range(3):
        for way, (slab, start, place) in enumerate(
            ((above, depth - HALO, 0), (below, 0, HALO + depth))
        ):
            class_sends.append(
                pltpu.make_async_remote_copy(
                    src_ref=labels_ref.at[pl.ds(start, HALO), chunk_rows[side], :],
                    dst_ref=classes.at[pl.ds(place, HALO), side],
                    send_sem=class_send.at[side, way],
                    recv_sem=class_recv.at[side, way],
                    device_id=(t, slab),
                    device_id_type=MESH,
                )
            )
    for copy in sends + class_sends:
        copy.start()

    row_number = lax.broadcasted_iota(jnp.int32, (8, width), 0)
    top, bottom = row_number == 0, row_number == 7
    upper = row_number < 4
    beta = alpha_wrap**0.25

    for copy in load_classes:
        copy.wait()
    for z in range(depth):
        rate = grain_rates(classes[HALO + z, 1], table_ref)
        real_part = 1.0 + diag_extra * rate
        scale = 1.0 / (real_part * real_part + beta * beta)
        coupling[0, z] = 1.0 / (real_part - beta)
        coupling[1, z] = 1.0 / (real_part + beta)
        coupling[2, z] = real_part * scale
        coupling[3, z] = -beta * scale
        coupling[4, z] = rate

    for copy in class_sends:
        copy.wait_recv()

    def swap(value):
        return pltpu.roll(value, 4, 0)

    def box_plane(z, carry):
        middle = swap(classes[z, 1])
        for part, label in enumerate(
            (
                jnp.where(upper, swap(classes[z, 0]), middle),
                jnp.where(upper, middle, swap(classes[z, 2])),
            )
        ):
            rate = grain_rates(label, table_ref)
            real_part = 1.0 + diag_extra * rate
            scale = rate / (real_part * real_part + beta * beta)
            rows = slice(8 * part, 8 * part + 8)
            box_coupling[0, z, rows] = rate / (real_part - beta)
            box_coupling[1, z, rows] = rate / (real_part + beta)
            box_coupling[2, z, rows] = real_part * scale
            box_coupling[3, z, rows] = beta * scale
        return carry

    lax.fori_loop(0, depth + 2 * HALO, box_plane, 0)

    load_first.wait()
    load_chunk.wait()
    load_rows.wait()
    for copy in sends:
        copy.wait_recv()

    def plane_neighbours(value, row_before, row_after):
        summed = jnp.where(top, row_before, pltpu.roll(value, 1, 0))
        summed += jnp.where(bottom, row_after, pltpu.roll(value, 7, 0))
        return summed + (pltpu.roll(value, 1, 1) + pltpu.roll(value, width - 1, 1))

    for z in range(depth):
        rate = coupling[4, z]
        scaled = []
        for n in range(4):
            value = chunk[n, z]
            around = plane_neighbours(
                value, rows_in[n, 0, z : z + 1, :], rows_in[n, 1, z : z + 1, :]
            )
            around += chunk[n, z - 1] if z > 0 else planes_in[n, 0]
            around += chunk[n, z + 1] if z < depth - 1 else planes_in[n, 1]
            earlier = chunk[n - 1, z] if n > 0 else first[z]
            laplacian = around - 6.0 * value
            residual = (
                value
                - earlier
                + tau_step * rate * (value * value * value - value - kappa_grad * laplacian)
            )
            scaled.append(residual * alpha_wrap ** (n / 4))
        even, odd = scaled[0] + scaled[2], scaled[1] + scaled[3]
        rhs_real, rhs_imag = scaled[0] - scaled[2], scaled[3] - scaled[1]
        inv_real, inv_imag = coupling[2, z], coupling[3, z]
        starts = (
            (even + odd) * coupling[0, z],
            (even - odd) * coupling[1, z],
            rhs_real * inv_real - rhs_imag * inv_imag,
            rhs_real * inv_imag + rhs_imag * inv_real,
        )
        for field in range(4):
            own[0, field, z] = starts[field]

    before, after = ring_place(lax.rem(p + 3, 4)), ring_place(lax.rem(p + 1, 4))

    def block_copies(block):
        moves = []
        for side, (slab, start) in enumerate(((above, depth - HALO), (below, 0))):
            moves.append(
                (own.at[block, :, pl.ds(start, HALO)], own_in.at[block, side], (t, slab))
            )
        for side, other in enumerate((after, before)):
            moves.append(
                (edges.at[block, side], edges_in.at[block, side], (other, s))
            )
            for slab, half, place in ((above, 1, 0), (below, 0, 1)):
                moves.append(
                    (
                        corners.at[block, side, half],
                        corners_in.at[block, side, place],
                        (other, slab),
                    )
                )
        return [
            pltpu.make_async_remote_copy(
                src_ref=source,
                dst_ref=target,
                send_sem=halo_send.at[block, number],
                recv_sem=halo_recv.at[block, number],
                device_id=device,
                device_id_type=MESH,
            )
            for number, (source, target, device) in enumerate(moves)
        ]

    def put_edges(block):
        def of_field(field, carry):
            for half in range(2):
                for i in range(2):
                    one = own[block, field, 4 * half + i]
                    two = own[block, field, 4 * half + i + 2]
                    edges[block, 0, half, field, i] = jnp.where(upper, swap(one), two)
                    edges[block, 1, half, field, i] = jnp.where(upper, one, swap(two))
            for half, nearest in enumerate(((0, 1, 2), (depth - 1, depth - 2, depth - 3))):
                one, two, three = (own[block, field, z] for z in nearest)
                two_three = jnp.where(row_number == 5, pltpu.roll(three, 6, 0), two)
                corners[block, 0, half, field] = jnp.where(upper, swap(one), two_three)
                two_three = jnp.where(row_number == 2, pltpu.roll(three, 2, 0), two)
                corners[block, 1, half, field] = jnp.where(upper, two_three, swap(one))
            return carry

        lax.fori_loop(0, 4, of_field, 0)

    def assemble(block, target):
        def of_field(field, carry):
            for z in range(depth + 2 * HALO):
                quarter, late, i = z // 4, z % 4 // 2, z % 2
                if quarter == 0:
                    middle = own_in[block, 0, field, z]
                elif quarter == 3:
                    middle = own_in[block, 1, field, z - HALO - depth]
                else:
                    middle = own[block, field, z - HALO]
                middle = swap(middle)
                if quarter in (0, 3):
                    away = HALO - z if quarter == 0 else z - HALO - depth + 1
                    low = corners_in[block, 0, quarter // 3, field]
                    high = corners_in[block, 1, quarter // 3, field]
                    if away == 2:
                        low, high = swap(low), swap(high)
                    if away == 3:
                        low, high = pltpu.roll(low, 6, 0), pltpu.roll(high, 2, 0)
                else:
                    low = edges_in[block, 0, quarter - 1, field, i]
                    high = edges_in[block, 1, quarter - 1, field, i]
                    low = swap(low) if late else low
                    high = high if late else swap(high)
                target[field, z, 0:8] = jnp.where(upper, low, middle)
                target[field, z, 8:16] = jnp.where(upper, middle, high)
            return carry

        lax.fori_loop(0, 4, of_field, 0)

    def sweep(source, target, first_plane, last_plane):
        def two_planes(pair, carry):
            for extra in range(2):
                z = first_plane + 2 * pair + extra
                sums = []
                for field in range(4):
                    value = source[field, z]
                    around = pltpu.roll(value, 1, 0) + pltpu.roll(value, 15, 0)
                    around += pltpu.roll(value, 1, 1) + pltpu.roll(value, width - 1, 1)
                    sums.append(around + (source[field, z - 1] + source[field, z + 1]))
                real, imag = box_coupling[2, z], box_coupling[3, z]
                target[0, z] = base[0, z] + box_coupling[0, z] * sums[0]
                target[1, z] = base[1, z] + box_coupling[1, z] * sums[1]
                target[2, z] = base[2, z] + real * sums[2] + imag * sums[3]
                target[3, z] = base[3, z] + real * sums[3] - imag * sums[2]
            return carry

        lax.fori_loop(0, (last_plane - first_plane) // 2, two_planes, 0)

    halos = []
    for block in range(BLOCKS):
        copies = block_copies(block)
        halos += copies
        for copy in copies[:2]:
            copy.start()
        put_edges(block)
        for number in (3, 4, 6, 7, 2, 5):
            copies[number].start()
        for copy in copies:
            copy.wait_recv()
        source = base if block == 0 else sol.at[0]
        assemble(block, source)
        for step in range(HALO):
            target = sol.at[(step + 1) % 2]
            sweep(source, target, step + 1, depth + 2 * HALO - 1 - step)
            source = target

        def take_own(field, carry):
            for z in range(depth):
                own[block + 1, field, z] = jnp.where(
                    upper,
                    swap(sol[0, field, HALO + z, 0:8]),
                    swap(sol[0, field, HALO + z, 8:16]),
                )
            return carry

        lax.fori_loop(0, 4, take_own, 0)

    for z in range(depth):
        zero, two, real, imag = (own[BLOCKS, field, z] for field in range(4))
        plus, minus = zero + two, zero - two
        back = (plus + 2.0 * real, minus - 2.0 * imag, plus - 2.0 * real, minus + 2.0 * imag)
        for n in range(4):
            result[n, z] = chunk[n, z] - back[n] * (0.25 * alpha_wrap ** (-n / 4))
    returns = []
    for ahead in (2, 1, 3):
        other = lax.rem(t + ahead, 4)
        returns.append(
            pltpu.make_async_remote_copy(
                src_ref=result.at[other],
                dst_ref=out_ref.at[:, my_rows, :],
                send_sem=back_send.at[ahead],
                recv_sem=back_recv.at[4 - ahead],
                device_id=(other, s),
                device_id_type=MESH,
            )
        )
    for copy in returns:
        copy.start()
    keep = pltpu.make_async_copy(result.at[t], out_ref.at[:, my_rows, :], local_sem.at[5])
    keep.start()
    for copy in sends + class_sends + halos:
        copy.wait_send()
    keep.wait()
    for copy in returns:
        copy.wait()


def fused_shards(state, initial, labels, mobility_table):
    _, depth, rows, width = state.shape
    slabs = lax.axis_size("space")
    f32 = jnp.float32
    dma = pltpu.SemaphoreType.DMA
    new_state = pl.pallas_call(
        functools.partial(paradiag_kernel, slabs),
        out_shape=jax.ShapeDtypeStruct((depth, rows, width), f32),
        in_specs=[pl.BlockSpec(memory_space=pltpu.SMEM)] + [pl.BlockSpec(memory_space=pltpu.HBM)] * 3,
        out_specs=pl.BlockSpec(memory_space=pltpu.VMEM),
        scratch_shapes=[
            pltpu.VMEM((depth, rows, width), f32),
            pltpu.VMEM((4, depth, 8, width), f32),
            pltpu.VMEM((depth, 8, width), f32),
            pltpu.VMEM((depth + 2 * HALO, 3, 8, width), jnp.int32),
            pltpu.VMEM((4, 2, depth, width), f32),
            pltpu.VMEM((4, 2, depth, width), f32),
            pltpu.VMEM((4, 2, 8, width), f32),
            pltpu.VMEM((5, depth, 8, width), f32),
            pltpu.VMEM((4, depth + 2 * HALO, 16, width), f32),
            pltpu.VMEM((4, depth + 2 * HALO, 16, width), f32),
            pltpu.VMEM((2, 4, depth + 2 * HALO, 16, width), f32),
            pltpu.VMEM((BLOCKS + 1, 4, depth, 8, width), f32),
            pltpu.VMEM((BLOCKS, 2, 4, HALO, 8, width), f32),
            pltpu.VMEM((BLOCKS, 2, 2, 4, 2, 8, width), f32),
            pltpu.VMEM((BLOCKS, 2, 2, 4, 2, 8, width), f32),
            pltpu.VMEM((BLOCKS, 2, 2, 4, 8, width), f32),
            pltpu.VMEM((BLOCKS, 2, 2, 4, 8, width), f32),
            pltpu.VMEM((4, depth, 8, width), f32),
            dma((9,)),
            dma((4,)),
            dma((4,)),
            dma((4,)),
            dma((4,)),
            dma((4, 2)),
            dma((4, 2)),
            dma((3, 2)),
            dma((3, 2)),
            dma((BLOCKS, 8)),
            dma((BLOCKS, 8)),
            dma((4,)),
            dma((4,)),
        ],
        compiler_params=pltpu.CompilerParams(
            collective_id=0, has_side_effects=True, vmem_limit_bytes=60 * 2**20
        ),
    )(mobility_table, state, initial, labels)
    return new_state[None]


def solution(mesh):
    in_specs = (P("tm", "space", None, None), P("space", None, None), P("space", None, None), P())
    out_specs = P("tm", "space", None, None)
    body = fused_shards if mesh.shape["tm"] == 4 and mesh.shape["space"] > 2 else shards
    return jax.shard_map(body, mesh=mesh, in_specs=in_specs, out_specs=out_specs, check_vma=False)
```
